512 devices in a mesh: section: 8 (over x, y_hi), seq: 64 (over z, y_lo, core).
Axes of the slice: x: 4, y: 8 (y_hi: 2, y_lo: 4; y = y_hi * 4 + y_lo), z: 8, core: 2. Of those that a mesh axis runs over, the one named last changes fastest.
Arguments:
- stream_in: bfloat16 [512, 1536], P('seq'), may hold values from -6 to 6
- head_maps: bfloat16 [8, 12, 128, 384], P('section'), may hold values from -0.5 to 0.5
- out_maps: bfloat16 [8, 12, 128, 128], P('section'), may hold values from -1.5 to 1.5
- norm_gains: float32 [8, 2, 128], P('section'), may hold values from 0.8 to 2.2
- modulation: float32 [8, 50, 3, 1536], P('section'), may hold values from -4 to 4
- stale_cache: bfloat16 [8, 2, 512, 3072], P('section', None, 'seq'), may hold values from -2.5 to 2.5
- patch_rows: int32 [8], replicated, may hold values from 0 to 7, each once
- stale_age: int32 [512], P('seq'), may hold values from 0 to 1
- timestep: int32 [1], replicated, may hold values from 0 to 49
Outputs:
- block_out: bfloat16 [8, 512, 1536], P('section', 'seq')
- fresh_cache: bfloat16 [8, 512, 3072], P('section', 'seq')
The draws below stay inside these ranges and needn't reach their ends.
Inputs may be any that keep to these rules, and one draw needn't show every extreme that they name: `patch_rows`: a permutation of the 8 local rows; entries p * 4 to (p + 1) * 4 - 1 name the rows of patch p.
All inputs are finite; a program needn't handle non-finite values.
Results may differ from the reference program's by a relative error of at most 0.019.
Values may be sent and summed in bfloat16 or wider, within the bound.
No kernel may reach another device: no remote copies, remote signals or barrier semaphores. Data moves between devices by JAX's collectives and lax.ppermute only.
A program may use at most 64 MiB of HBM per device.

```python
import math
import jax
import jax.numpy as jnp
from jax import lax

HEADS = 12
HEAD_DIM = 128
WIDTH = 1536
PATCHES = 2
PATCH_ROWS = 4
LOCAL_ROWS = 8
SEQ_TOKENS = 512
BLOCKS = 8
CACHE_AGES = 2
SCHED_STEPS = 50
N_SEQ = 64


def set_ends(array, rng, low, largest):
    shape = array.shape
    spot = [jax.random.randint(jax.random.fold_in(rng, axis), (), 0, shape[axis]) for axis in range(len(shape))]
    array = array.at[tuple(spot)].set(low)
    longest = shape.index(max(shape))
    spot[longest] = (spot[longest] + 1) % shape[longest]
    return array.at[tuple(spot)].set(largest)


def shard_levels(stream_key, dims, pieces, smallest, largest):
    def one(dim, shards_of):
        draws = jax.random.uniform(jax.random.fold_in(jax.random.fold_in(stream_key, 6), dim), (shards_of,), jnp.float32, smallest / len(pieces), largest / len(pieces))
        return jnp.repeat(jnp.exp(draws), dims[dim] // shards_of).reshape((-1,) + (1,) * (len(dims) - dim - 1))

    factor_of = one(*pieces[0])
    for cut in pieces[1:]:
        factor_of = factor_of * one(*cut)
    return factor_of


def centred(rng, dims, deviation, most, pieces=(), kind=jnp.bfloat16):
    entries = deviation * jax.random.normal(rng, dims, jnp.float32)
    if pieces:
        entries = entries * shard_levels(rng, dims, pieces, -0.22, 0.18)
    return jnp.clip(entries, -most, most).astype(kind)


def setup_inputs(seed: int = 0) -> dict:
    keys = jax.random.split(jax.random.key(seed), 10)
    stream_in = centred(keys[0], (SEQ_TOKENS, WIDTH), 1.0, 6.0, ((0, 64),))
    head_maps = centred(keys[1], (BLOCKS, HEADS, HEAD_DIM, 3 * HEAD_DIM), HEAD_DIM ** -0.5, 0.5, ((0, 8),))
    out_maps = centred(keys[2], (BLOCKS, HEADS, HEAD_DIM, HEAD_DIM), (HEAD_DIM // 8) ** -0.5, 1.5, ((0, 8),))
    norm_gains = jnp.clip(jnp.exp(math.log(2.2) - 1.011601 * jax.random.uniform(keys[3], (BLOCKS, 2, HEAD_DIM), jnp.float32) ** shard_levels(keys[3], (BLOCKS, 2, HEAD_DIM), ((0, 8),), -0.2, 0.2)), 0.8, 2.2)
    modulation = centred(keys[4], (BLOCKS, SCHED_STEPS, 3, WIDTH), 1.0, 4.0, ((0, 8),), jnp.float32)
    stale_cache = centred(keys[5], (BLOCKS, CACHE_AGES, SEQ_TOKENS, 2 * WIDTH), 1.0, 2.5, ((0, 8), (2, 64)))
    patch_rows = jax.random.permutation(keys[6], LOCAL_ROWS).astype(jnp.int32)
    stale_age = set_ends(jax.random.randint(keys[7], (SEQ_TOKENS,), 0, CACHE_AGES), jax.random.fold_in(keys[7], 1), 0, CACHE_AGES - 1).astype(jnp.int32)
    timestep = jax.random.randint(keys[8], (1,), 0, SCHED_STEPS).astype(jnp.int32)
    return dict(stream_in=stream_in, head_maps=head_maps, out_maps=out_maps, norm_gains=norm_gains, modulation=modulation, stale_cache=stale_cache, patch_rows=patch_rows, stale_age=stale_age, timestep=timestep)


def head_norm(projected, gains):
    scaled = projected * lax.rsqrt(lax.optimization_barrier(jnp.mean(projected * projected, axis=-1, keepdims=True)) + 1e-06) * gains
    return scaled.astype(jnp.bfloat16)

def reference(stream_in, head_maps, out_maps, norm_gains, modulation, stale_cache, patch_rows, stale_age, timestep):
    row_order = jnp.arange(LOCAL_ROWS, dtype=jnp.int32)
    matches = (patch_rows[:, None] == row_order[None, :]).astype(jnp.int32)
    local_patch = lax.optimization_barrier(jnp.sum(matches * (row_order[:, None] // PATCH_ROWS), axis=0)).astype(jnp.int32)
    row_patch = jnp.tile(local_patch, N_SEQ)
    row_age = stale_age.astype(jnp.int32)
    device_base = (jnp.arange(N_SEQ, dtype=jnp.int32) * LOCAL_ROWS)[:, None]
    scale_factor = HEAD_DIM ** (-0.5)
    current = stream_in
    outputs = []
    caches = []
    for block_id in range(BLOCKS):
        mod_row = modulation[block_id, timestep[0]]
        stale_sel = stale_cache[block_id, 0]
        for age_id in range(1, CACHE_AGES):
            stale_sel = jnp.where((row_age == age_id)[:, None], stale_cache[block_id, age_id], stale_sel)
        fresh = jnp.zeros((SEQ_TOKENS, 2 * WIDTH), jnp.bfloat16)
        result = jnp.zeros((SEQ_TOKENS, WIDTH), jnp.bfloat16)
        for patch_id in range(PATCHES):
            chosen = patch_rows[patch_id * PATCH_ROWS:(patch_id + 1) * PATCH_ROWS]
            row_ids = (device_base + chosen[None, :]).reshape(-1).astype(jnp.int32)
            count_rows = row_ids.shape[0]
            stream_rows = current[row_ids].astype(jnp.float32)
            center = lax.optimization_barrier(jnp.mean(stream_rows, axis=-1, keepdims=True))
            spread = lax.optimization_barrier(jnp.mean(jnp.square(stream_rows - center), axis=-1, keepdims=True))
            normed = (stream_rows - center) * lax.rsqrt(spread + 1e-06)
            mod_rows = lax.optimization_barrier((normed * (1.0 + mod_row[1]) + mod_row[0]).astype(jnp.bfloat16))
            projected = jnp.einsum('rhc,hcd->rhd', mod_rows.reshape(count_rows, HEADS, HEAD_DIM).astype(jnp.float32), head_maps[block_id].astype(jnp.float32))
            queries = lax.optimization_barrier(head_norm(projected[..., :HEAD_DIM], norm_gains[block_id, 0]))
            key_part = head_norm(projected[..., HEAD_DIM:2 * HEAD_DIM], norm_gains[block_id, 1]).reshape(count_rows, WIDTH)
            value_part = projected[..., 2 * HEAD_DIM:].astype(jnp.bfloat16).reshape(count_rows, WIDTH)
            fresh = fresh.at[row_ids].set(jnp.concatenate([key_part, value_part], axis=1))
            key_value = lax.optimization_barrier(jnp.where((row_patch <= patch_id)[:, None], fresh, stale_sel))
            key_rows = key_value[:, :WIDTH].reshape(SEQ_TOKENS, HEADS, HEAD_DIM).astype(jnp.float32)
            value_rows = key_value[:, WIDTH:].reshape(SEQ_TOKENS, HEADS, HEAD_DIM).astype(jnp.float32)
            scores = jnp.einsum('rhc,nhc->hrn', queries.astype(jnp.float32), key_rows) * scale_factor
            weights = jnp.exp(scores)
            denominator = lax.optimization_barrier(jnp.sum(weights, axis=2))
            rounded = lax.optimization_barrier(weights.astype(jnp.bfloat16))
            numerator = jnp.einsum('hrn,nhc->rhc', rounded.astype(jnp.float32), value_rows)
            attended = lax.optimization_barrier((numerator / jnp.transpose(denominator)[:, :, None]).astype(jnp.bfloat16))
            branch = jnp.einsum('rhc,hcd->rhd', attended.astype(jnp.float32), out_maps[block_id].astype(jnp.float32)).reshape(count_rows, WIDTH)
            out_rows = (stream_rows + mod_row[2] * branch).astype(jnp.bfloat16)
            result = result.at[row_ids].set(out_rows)
        outputs.append(result)
        caches.append(fresh)
        current = result
    return (jnp.stack(outputs), jnp.stack(caches))
```

```python
import math

import jax
import jax.numpy as jnp
from jax import lax
from jax.experimental import pallas as pl
from jax.experimental.pallas import tpu as pltpu
from jax.sharding import Mesh
from jax.sharding import PartitionSpec as P

HEAD_DIM = 128
EPS = 1e-06
QUERY_SCALE = HEAD_DIM ** (-0.5) * math.log2(math.e)
VMEM = pl.BlockSpec(memory_space=pltpu.VMEM)
PARAMS = pltpu.CompilerParams(vmem_limit_bytes=32 * 2**20)


def row_to_columns(first, second):
    rows = lax.broadcasted_iota(jnp.int32, (HEAD_DIM, first.shape[1]), 0)
    return jnp.transpose(jnp.where(rows == 0, first, second))


def half_stats(pieces):
    width = len(pieces) * HEAD_DIM
    total = pieces[0]
    for piece in pieces[1:]:
        total = total + piece
    center = jnp.sum(total, axis=1, keepdims=True) * (1.0 / width)
    squares = jnp.square(pieces[0] - center)
    for piece in pieces[1:]:
        squares = squares + jnp.square(piece - center)
    spread = jnp.sum(squares, axis=1, keepdims=True)
    lanes = lax.broadcasted_iota(jnp.int32, squares.shape, 1)
    return jnp.transpose(jnp.where(lanes == 0, center, spread))[:8]


def head_slices(width):
    return [slice(h * HEAD_DIM, (h + 1) * HEAD_DIM) for h in range(width // HEAD_DIM)]


def stats_kernel(x0_ref, x1_ref, st0_ref, st1_ref):
    for x_ref, st_ref in ((x0_ref, st0_ref), (x1_ref, st1_ref)):
        cuts = head_slices(x_ref.shape[1])
        st_ref[...] = half_stats([x_ref[:, cut].astype(jnp.float32) for cut in cuts])


def first_stats(x0, x1):
    tokens = x0.shape[0]
    return pl.pallas_call(
        stats_kernel,
        out_shape=(jax.ShapeDtypeStruct((8, tokens), jnp.float32),) * 2,
        in_specs=[VMEM] * 2,
        out_specs=(VMEM,) * 2,
        compiler_params=PARAMS,
        name="first_stats",
    )(x0, x1)


def scores(left, right):
    return lax.dot_general(
        left, right, (((1,), (1,)), ((), ())), preferred_element_type=jnp.float32
    )


def unit_norm(part):
    return part * lax.rsqrt(jnp.mean(part * part, axis=1, keepdims=True) + EPS)


def block_kernel(
    x_ref, st_ref, par_ref, w_ref, ok_ref, ov_ref, xo_ref, k_ref, v_ref, so_ref
):
    width = x_ref.shape[1]
    mean_a, dev_a = (st_ref[0, 0:1], st_ref[0, 1:2])
    mean_b, dev_b = (st_ref[1, 0:1], st_ref[1, 1:2])
    mean = 0.5 * (mean_a + mean_b)
    spread = (dev_a + dev_b + jnp.square(mean_a - mean_b) * (0.5 * width)) * (0.5 / width)
    columns = row_to_columns(mean, lax.rsqrt(spread + EPS))
    mean, rstd = (columns[:, 0:1], columns[:, 1:2])
    query_gain = par_ref[3:4, :HEAD_DIM] * QUERY_SCALE
    key_gain = par_ref[3:4, HEAD_DIM : 2 * HEAD_DIM]
    results = []
    for head, cut in enumerate(head_slices(width)):
        x = x_ref[:, cut].astype(jnp.float32)
        mod_in = (x - mean) * rstd * (1.0 + par_ref[1:2, cut]) + par_ref[0:1, cut]
        projected = jnp.dot(
            mod_in.astype(jnp.bfloat16),
            w_ref[head, :, : 3 * HEAD_DIM],
            preferred_element_type=jnp.float32,
        )
        query = (unit_norm(projected[:, :HEAD_DIM]) * query_gain).astype(jnp.bfloat16)
        key = (unit_norm(projected[:, HEAD_DIM : 2 * HEAD_DIM]) * key_gain).astype(jnp.bfloat16)
        value = projected[:, 2 * HEAD_DIM :].astype(jnp.bfloat16)
        k_ref[:, cut] = key
        v_ref[:, cut] = value
        fresh = jnp.exp2(scores(query, key))
        other = jnp.exp2(scores(query, ok_ref[:, cut]))
        total = jnp.sum(fresh + other, axis=1, keepdims=True)
        numerator = jnp.dot(
            fresh.astype(jnp.bfloat16), value, preferred_element_type=jnp.float32
        ) + jnp.dot(
            other.astype(jnp.bfloat16), ov_ref[:, cut], preferred_element_type=jnp.float32
        )
        attended = (numerator / total).astype(jnp.bfloat16)
        branch = jnp.dot(
            attended, w_ref[head, :, 3 * HEAD_DIM :], preferred_element_type=jnp.float32
        )
        x_out = (x + par_ref[2:3, cut] * branch).astype(jnp.bfloat16)
        xo_ref[:, cut] = x_out
        results.append(x_out.astype(jnp.float32))
    so_ref[...] = half_stats(results)


def block_step(x, stats, params, weights, other_keys, other_values):
    tokens, width = x.shape
    return pl.pallas_call(
        block_kernel,
        out_shape=(jax.ShapeDtypeStruct((tokens, width), jnp.bfloat16),) * 3
        + (jax.ShapeDtypeStruct((8, tokens), jnp.float32),),
        in_specs=[VMEM] * 6,
        out_specs=(VMEM,) * 4,
        compiler_params=PARAMS,
        cost_estimate=pl.CostEstimate(
            flops=2_000_000_000, bytes_accessed=4_000_000, transcendentals=800_000
        ),
        name="block_step",
    )(x, stats, params, weights, other_keys, other_values)


def swap_copies(array, axis):
    count = lax.axis_size(axis)
    copies = jnp.broadcast_to(array[None], (count,) + array.shape)
    return lax.all_to_all(copies, axis, split_axis=0, concat_axis=0, tiled=True)


def shards(
    stream_in,
    head_maps,
    out_maps,
    norm_gains,
    modulation,
    stale_cache,
    patch_rows,
    stale_age,
    timestep,
):
    local, width = stream_in.shape
    heads = head_maps.shape[1]
    half = width // 2
    rows = local // 2
    planes = lax.axis_size("x")
    z_count, yl_count = (lax.axis_size("z"), lax.axis_size("yl"))
    pairs = z_count * yl_count
    core, plane, upper = (lax.axis_index("c"), lax.axis_index("x"), lax.axis_index("yh"))
    pair = lax.axis_index("yl") * z_count + lax.axis_index("z")
    tokens = pairs * 2 * rows

    order = (patch_rows[:, None] == jnp.arange(local)[None, :]).astype(jnp.bfloat16)
    stale = jnp.where((stale_age == 1)[:, None], stale_cache[0, 1], stale_cache[0, 0])
    later = jnp.dot(order[rows:], stale).reshape(rows, 2, 2, half)
    stream_order = lax.dynamic_slice_in_dim(order, upper * rows, rows)
    stream = jnp.dot(stream_order, stream_in).reshape(rows, 1, 2, half)
    halves = jnp.transpose(jnp.concatenate([later, stream], axis=1), (2, 1, 0, 3))
    halves = lax.all_to_all(halves, "c", split_axis=0, concat_axis=0, tiled=True)
    mine = jnp.transpose(halves, (1, 0, 2, 3)).reshape(6 * rows, half)
    share = half // pairs
    first = core * half + pair * share
    cut = jnp.concatenate(
        [
            lax.dynamic_slice_in_dim(
                head_maps[0].reshape(heads * HEAD_DIM, 3 * HEAD_DIM), first, share
            ),
            lax.dynamic_slice_in_dim(out_maps[0].reshape(heads * HEAD_DIM, HEAD_DIM), first, share),
        ],
        axis=1,
    )
    tiles = jnp.transpose(cut.reshape(share // 8, 8, 4, HEAD_DIM), (0, 2, 1, 3))
    lanes = half // HEAD_DIM
    tiles = jnp.transpose(tiles.reshape(-1, lanes, 8, HEAD_DIM), (0, 2, 1, 3)).reshape(-1, half)
    given = jnp.concatenate([mine, tiles], axis=0)
    given_rows = given.shape[0]
    taken = lax.all_gather(swap_copies(given, "z"), ("yh", "yl"), axis=0, tiled=False)
    taken = taken.reshape(2, yl_count, z_count, given_rows, half)

    mod = lax.dynamic_index_in_dim(modulation[0], timestep[0], 0, keepdims=False)
    mod = lax.dynamic_slice_in_dim(mod, core * half, half, axis=1)
    gains = jnp.pad(norm_gains[0].reshape(1, 2 * HEAD_DIM), ((0, 0), (0, half - 2 * HEAD_DIM)))
    params = lax.all_gather(jnp.concatenate([mod, gains], axis=0), "yh", axis=0, tiled=False)

    span = 2 * rows
    stale_keys, stale_values, weights, current = ([], [], [], [])
    for block in range(2):
        here = taken[block]
        stale_keys.append(here[:, :, :span].reshape(tokens, half))
        stale_values.append(here[:, :, span : 2 * span].reshape(tokens, half))
        current.append(here[:, :, 2 * span : 3 * span].reshape(tokens, half))
        packed = here[:, :, 3 * span :].reshape(pairs, -1, 8, lanes, HEAD_DIM)
        packed = jnp.transpose(packed, (0, 1, 3, 2, 4)).reshape(pairs, share // 8, 4, 8, HEAD_DIM)
        packed = jnp.transpose(packed, (0, 1, 3, 2, 4))
        weights.append(packed.reshape(half // HEAD_DIM, HEAD_DIM, 4 * HEAD_DIM))

    stats = [lax.all_gather(part, "c", axis=0) for part in first_stats(*current)]
    kept = None
    for turn in range(planes):
        own = [[], []]
        fresh = [None, None]
        for patch in range(2):
            x, stat = (current[patch], stats[patch])
            for block in range(2):
                keys, values = (
                    (stale_keys[block], stale_values[block]) if patch == 0 else fresh[block]
                )
                x, new_keys, new_values, part = block_step(
                    x, stat, params[block], weights[block], keys, values
                )
                fresh[block] = (new_keys, new_values)
                stat = lax.all_gather(part, "c", axis=0)
                own[block] += [
                    lax.dynamic_slice_in_dim(array, pair * span, span)
                    for array in (new_keys, new_values, x)
                ]
            if turn < planes - 1:
                hop = [(turn, turn + 1)]
                current[patch] = lax.ppermute(x, "x", hop)
                stats[patch] = lax.ppermute(stat, "x", hop)
        found = jnp.where(upper == 0, jnp.stack(own[0]), jnp.stack(own[1]))
        kept = found if kept is None else jnp.where(plane == turn, found, kept)

    kept = jnp.transpose(kept.reshape(2, 3, 2, rows, half), (2, 0, 1, 3, 4))
    kept = lax.all_to_all(kept, "c", split_axis=0, concat_axis=0, tiled=True)
    kept = jnp.transpose(kept, (1, 3, 2, 0, 4)).reshape(local, 3 * width)
    kept = lax.dot_general(order, kept, (((0,), (0,)), ((), ())))
    return (kept[None, :, 2 * width :], kept[None, :, : 2 * width])


def solution(mesh):
    fine = Mesh(mesh.devices.reshape(4, 2, 8, 4, 2), ("x", "yh", "z", "yl", "c"))
    section, seq = (("x", "yh"), ("z", "yl", "c"))
    in_specs = (
        P(seq, None),
        P(section, None, None, None),
        P(section, None, None, None),
        P(section, None, None),
        P(section, None, None, None),
        P(section, None, seq, None),
        P(),
        P(seq),
        P(),
    )
    out_specs = (P(section, seq, None), P(section, seq, None))
    return jax.shard_map(shards, mesh=fine, in_specs=in_specs, out_specs=out_specs, check_vma=False)
```

```python
import math

import jax
import jax.numpy as jnp
from jax import lax
from jax.experimental import pallas as pl
from jax.experimental.pallas import tpu as pltpu
from jax.sharding import Mesh
from jax.sharding import PartitionSpec as P

HEAD_DIM = 128
EPS = 1e-06
QUERY_SCALE = HEAD_DIM ** (-0.5) * math.log2(math.e)
VMEM = pl.BlockSpec(memory_space=pltpu.VMEM)
STAT_ROWS = 16
SEQ = ("z", "yl", "c")
PARAMS = pltpu.CompilerParams(vmem_limit_bytes=32 * 2**20)


def row_to_columns(first, second):
    rows = lax.broadcasted_iota(jnp.int32, (HEAD_DIM, first.shape[1]), 0)
    return jnp.transpose(jnp.where(rows == 0, first, second))


def split_rows(row):
    parts = []
    for _ in range(3):
        part = row.astype(jnp.bfloat16).astype(jnp.float32)
        parts.append(part)
        row = row - part
    return parts


def half_stats(pieces):
    width = len(pieces) * HEAD_DIM
    total = pieces[0]
    for piece in pieces[1:]:
        total = total + piece
    center = jnp.sum(total, axis=1, keepdims=True) * (1.0 / width)
    squares = jnp.square(pieces[0] - center)
    for piece in pieces[1:]:
        squares = squares + jnp.square(piece - center)
    spread = jnp.sum(squares, axis=1, keepdims=True)
    lanes = lax.broadcasted_iota(jnp.int32, squares.shape, 1)
    both = jnp.transpose(jnp.where(lanes == 0, center, spread))
    rows = lax.broadcasted_iota(jnp.int32, (STAT_ROWS, both.shape[1]), 0)
    packed = jnp.zeros(rows.shape, jnp.float32)
    for index, part in enumerate(split_rows(both[0:1]) + split_rows(both[1:2])):
        packed = jnp.where(rows == index, part, packed)
    return packed.astype(jnp.bfloat16)


def head_slices(width):
    return [slice(h * HEAD_DIM, (h + 1) * HEAD_DIM) for h in range(width // HEAD_DIM)]


def stats_kernel(x0_ref, x1_ref, st_ref):
    for index, x_ref in enumerate((x0_ref, x1_ref)):
        cuts = head_slices(x_ref.shape[1])
        st_ref[index] = half_stats([x_ref[:, cut].astype(jnp.float32) for cut in cuts])


def first_stats(x0, x1):
    tokens = x0.shape[0]
    return pl.pallas_call(
        stats_kernel,
        out_shape=jax.ShapeDtypeStruct((2, STAT_ROWS, tokens), jnp.bfloat16),
        in_specs=[VMEM] * 2,
        out_specs=VMEM,
        compiler_params=PARAMS,
        name="first_stats",
    )(x0, x1)


def scores(left, right):
    return lax.dot_general(
        left, right, (((1,), (1,)), ((), ())), preferred_element_type=jnp.float32
    )


def unit_norm(part):
    return part * lax.rsqrt(jnp.mean(part * part, axis=1, keepdims=True) + EPS)


def block_kernel(x_ref, st_ref, par_ref, w_ref, ok_ref, ov_ref, xo_ref, k_ref, v_ref):
    tokens, width = k_ref.shape

    def joined(core, first):
        parts = [st_ref[core, first + i : first + i + 1].astype(jnp.float32) for i in range(3)]
        return parts[0] + parts[1] + parts[2]

    mean_a, mean_b = (joined(0, 0), joined(1, 0))
    spread = joined(0, 3) + joined(1, 3) + jnp.square(mean_a - mean_b) * (0.5 * width)
    columns = row_to_columns(
        0.5 * (mean_a + mean_b), lax.rsqrt(spread * (0.5 / width) + EPS)
    )
    mean, rstd = (columns[:, 0:1], columns[:, 1:2])
    query_gain = par_ref[3:4, :HEAD_DIM] * QUERY_SCALE
    key_gain = par_ref[3:4, HEAD_DIM : 2 * HEAD_DIM]
    results = []
    for head, cut in enumerate(head_slices(width)):
        x = x_ref[:tokens, cut].astype(jnp.float32)
        mod_in = (x - mean) * rstd * (1.0 + par_ref[1:2, cut]) + par_ref[0:1, cut]
        projected = jnp.dot(
            mod_in.astype(jnp.bfloat16),
            w_ref[head, :, : 3 * HEAD_DIM],
            preferred_element_type=jnp.float32,
        )
        query = (unit_norm(projected[:, :HEAD_DIM]) * query_gain).astype(jnp.bfloat16)
        key = (unit_norm(projected[:, HEAD_DIM : 2 * HEAD_DIM]) * key_gain).astype(jnp.bfloat16)
        value = projected[:, 2 * HEAD_DIM :].astype(jnp.bfloat16)
        k_ref[:, cut] = key
        v_ref[:, cut] = value
        fresh = jnp.exp2(scores(query, key))
        other = jnp.exp2(scores(query, ok_ref[:, cut]))
        total = jnp.sum(fresh + other, axis=1, keepdims=True)
        numerator = jnp.dot(
            fresh.astype(jnp.bfloat16), value, preferred_element_type=jnp.float32
        ) + jnp.dot(
            other.astype(jnp.bfloat16), ov_ref[:, cut], preferred_element_type=jnp.float32
        )
        attended = (numerator / total).astype(jnp.bfloat16)
        branch = jnp.dot(
            attended, w_ref[head, :, 3 * HEAD_DIM :], preferred_element_type=jnp.float32
        )
        x_out = (x + par_ref[2:3, cut] * branch).astype(jnp.bfloat16)
        xo_ref[:tokens, cut] = x_out
        results.append(x_out.astype(jnp.float32))
    xo_ref[tokens:, :tokens] = half_stats(results)
    xo_ref[tokens:, tokens:] = jnp.zeros((STAT_ROWS, width - tokens), jnp.bfloat16)


def block_step(x, stats, block, keys, values):
    params, weights = block
    tokens, width = keys.shape
    return pl.pallas_call(
        block_kernel,
        out_shape=(
            jax.ShapeDtypeStruct((tokens + STAT_ROWS, width), jnp.bfloat16),
            jax.ShapeDtypeStruct((tokens, width), jnp.bfloat16),
            jax.ShapeDtypeStruct((tokens, width), jnp.bfloat16),
        ),
        in_specs=[VMEM] * 6,
        out_specs=(VMEM,) * 3,
        compiler_params=PARAMS,
        cost_estimate=pl.CostEstimate(
            flops=1_000_000, bytes_accessed=100_000, transcendentals=1_000
        ),
        name="block_step",
    )(x, stats, params, weights, keys, values)


def shards(
    stream_in,
    head_maps,
    out_maps,
    norm_gains,
    modulation,
    stale_cache,
    patch_rows,
    stale_age,
    timestep,
):
    local, width = stream_in.shape
    heads = head_maps.shape[1]
    half = width // 2
    rows = local // 2
    span = 2 * rows
    planes, yl_count = (lax.axis_size("x"), lax.axis_size("yl"))
    z_count, seq_count = (lax.axis_size("z"), lax.axis_size(SEQ))
    core, plane, upper = (lax.axis_index("c"), lax.axis_index("x"), lax.axis_index("yh"))
    z, yl = (lax.axis_index("z"), lax.axis_index("yl"))
    tokens = seq_count * rows
    low = yl == 0

    def spot(x, yh, y):
        return (x * 2 + yh) * yl_count + y

    def send(array, pairs):
        return lax.ppermute(array, ("x", "yh", "yl"), pairs)

    last = yl_count - 1
    climb = [(0, last), (last, 0)]

    order = (patch_rows[:, None] == jnp.arange(local)[None, :]).astype(jnp.bfloat16)
    stale = jnp.where((stale_age == 1)[:, None], stale_cache[0, 1], stale_cache[0, 0])
    later = jnp.dot(order[rows:], stale).reshape(rows, 2, 2, half)
    stream = jnp.dot(order, stream_in).reshape(2, rows, 2, half)
    given = jnp.concatenate(
        [jnp.transpose(later, (2, 1, 0, 3)), jnp.transpose(stream, (2, 0, 1, 3))], axis=1
    )
    given = jnp.broadcast_to(given[None], (seq_count // 2,) + given.shape)
    given = given.reshape((seq_count,) + given.shape[2:])
    taken = lax.all_to_all(given, SEQ, split_axis=0, concat_axis=0, tiled=True)
    keys, values, x0, x1 = [taken[:, i].reshape(tokens, half) for i in range(4)]

    mod = lax.dynamic_index_in_dim(modulation[0], timestep[0], 0, keepdims=False)
    mod = lax.dynamic_slice_in_dim(mod, core * half, half, axis=1)
    gains = jnp.pad(norm_gains[0].reshape(1, 2 * HEAD_DIM), ((0, 0), (0, half - 2 * HEAD_DIM)))
    params = jnp.concatenate([mod, gains], axis=0)
    weights = jnp.concatenate(
        [
            lax.dynamic_slice_in_dim(head_maps[0], core * (heads // 2), heads // 2),
            lax.dynamic_slice_in_dim(out_maps[0], core * (heads // 2), heads // 2),
        ],
        axis=2,
    )
    own = (params, weights)
    lift = [(spot(x, 0, a), spot(x, 1, b)) for x in range(1, planes) for a, b in climb]
    under_params, x0 = lax.optimization_barrier((send(params, lift), x0))
    under = (under_params, send(weights, lift))
    under_keys, under_values = (send(keys, lift), send(values, lift))

    def join(x):
        return lax.all_gather(x[tokens:, :tokens], "c", axis=0)

    def piece(arrays, y):
        at = (z * yl_count + y) * span
        return jnp.stack([lax.dynamic_slice_in_dim(array, at, span) for array in arrays])

    beside, far = (jnp.where(low, 1, last - 1), jnp.where(low, last - 1, 1))
    across = jnp.where(low, last, 0)

    stats = lax.all_gather(first_stats(x0, x1), "c", axis=0)
    current, stats = ([x0, x1], [stats[:, 0], stats[:, 1]])
    found = []
    for step in range(2):
        if step == 0:
            hop = [(spot(0, 0, a), spot(0, 1, b)) for a, b in climb]
        else:
            hop = [(spot(0, 1, y), spot(1, 1, y)) for y in (0, last)]
        done, others = ([], (keys, values))
        for patch in range(2):
            if patch == 1:
                current[1], x = lax.optimization_barrier((current[1], x))
            stat = join(current[patch]) if step else stats[patch]
            x, *others = block_step(current[patch], stat, own, *others)
            current[patch] = send(x, hop)
            done += [*others, x]
        found.append((piece(done, yl), piece(done, beside)))
    mine, near = [jnp.where(upper == 0, a, b) for a, b in zip(*found)]

    down = None
    for turn in range(1, planes):
        fresh = [(under_keys, under_values), (keys, values)]
        done = [[], []]
        hop = [(spot(turn, 1, y), spot(turn + 1, 1, y)) for y in (0, last)]
        for patch in range(2):
            if patch == 1:
                current[1], x = lax.optimization_barrier((current[1], x))
            x = current[patch]
            for index, block in enumerate((under, own)):
                x, *fresh[index] = block_step(x, join(x), block, *fresh[index])
                done[index] += [*fresh[index], x]
            if turn < planes - 1:
                current[patch] = send(x, hop)
        here = plane == turn
        new = (piece(done[0], across), piece(done[0], far))
        down = new if down is None else [jnp.where(here, a, b) for a, b in zip(new, down)]
        mine = jnp.where(here, piece(done[1], yl), mine)
        near = jnp.where(here, piece(done[1], beside), near)

    inner = [(0, 1), (last, last - 1)]
    spread = [(spot(x, 1, a), spot(x, 1, b)) for x in range(planes) for a, b in inner]
    spread += [(spot(0, 0, a), spot(0, 0, b)) for a, b in inner]
    descend = [(spot(x, 1, a), spot(x, 0, b)) for x in range(1, planes) for a, b in climb]
    reach = [(0, last - 1), (last, 1)]
    beyond = [(spot(x, 1, a), spot(x, 0, b)) for x in range(1, planes) for a, b in reach]
    got = jnp.where(
        jnp.logical_or(plane == 0, upper == 1),
        send(near, spread),
        jnp.where(jnp.logical_or(low, yl == last), send(down[0], descend), send(down[1], beyond)),
    )
    local_site = jnp.logical_and(
        jnp.logical_or(plane == 0, upper == 1), jnp.logical_or(low, yl == last)
    )
    kept = jnp.where(local_site, mine, got)

    kept = jnp.transpose(kept.reshape(2, 3, 2, rows, half), (2, 0, 1, 3, 4))
    kept = lax.all_to_all(kept, "c", split_axis=0, concat_axis=0, tiled=True)
    kept = jnp.transpose(kept, (1, 3, 2, 0, 4)).reshape(local, 3 * width)
    kept = lax.dot_general(order, kept, (((0,), (0,)), ((), ())))
    return (kept[None, :, 2 * width :], kept[None, :, : 2 * width])


def solution(mesh):
    fine = Mesh(mesh.devices.reshape(4, 2, 8, 4, 2), ("x", "yh", "z", "yl", "c"))
    section, seq = (("x", "yh"), SEQ)
    in_specs = (
        P(seq, None),
        P(section, None, None, None),
        P(section, None, None, None),
        P(section, None, None),
        P(section, None, None, None),
        P(section, None, seq, None),
        P(),
        P(seq),
        P(),
    )
    out_specs = (P(section, seq, None), P(section, seq, None))
    return jax.shard_map(shards, mesh=fine, in_specs=in_specs, out_specs=out_specs, check_vma=False)
```

```python
import math

import jax
import jax.numpy as jnp
from jax import lax
from jax.experimental import pallas as pl
from jax.experimental.pallas import tpu as pltpu
from jax.sharding import Mesh
from jax.sharding import PartitionSpec as P

HEAD_DIM = 128
EPS = 1e-06
QUERY_SCALE = HEAD_DIM ** (-0.5) * math.log2(math.e)
VMEM = pl.BlockSpec(memory_space=pltpu.VMEM)
STAT_ROWS = 16
SEQ = ("z", "yl", "c")
PARAMS = pltpu.CompilerParams(vmem_limit_bytes=32 * 2**20)


def row_to_columns(first, second):
    rows = lax.broadcasted_iota(jnp.int32, (HEAD_DIM, first.shape[1]), 0)
    return jnp.transpose(jnp.where(rows == 0, first, second))


def split_rows(row):
    parts = []
    for _ in range(3):
        part = row.astype(jnp.bfloat16).astype(jnp.float32)
        parts.append(part)
        row = row - part
    return parts


def half_stats(pieces):
    width = len(pieces) * HEAD_DIM
    total = pieces[0]
    for piece in pieces[1:]:
        total = total + piece
    center = jnp.sum(total, axis=1, keepdims=True) * (1.0 / width)
    squares = jnp.square(pieces[0] - center)
    for piece in pieces[1:]:
        squares = squares + jnp.square(piece - center)
    spread = jnp.sum(squares, axis=1, keepdims=True)
    lanes = lax.broadcasted_iota(jnp.int32, squares.shape, 1)
    both = jnp.transpose(jnp.where(lanes == 0, center, spread))
    rows = lax.broadcasted_iota(jnp.int32, (STAT_ROWS, both.shape[1]), 0)
    packed = jnp.zeros(rows.shape, jnp.float32)
    for index, part in enumerate(split_rows(both[0:1]) + split_rows(both[1:2])):
        packed = jnp.where(rows == index, part, packed)
    return packed.astype(jnp.bfloat16)


def head_slices(width):
    return [slice(h * HEAD_DIM, (h + 1) * HEAD_DIM) for h in range(width // HEAD_DIM)]


def offer_kernel(age_ref, rows_ref, half_ref, stale_ref, stream_ref, out_ref, stale_rows, stream_rows):
    local = stream_ref.shape[0]
    rows = local // 2
    width = stream_ref.shape[1] // 2
    fold = 3 * width // 2
    rest = fold - width
    index = lax.broadcasted_iota(jnp.int32, (local, 1), 0)
    newer = jnp.zeros((local, 1), jnp.int32)
    for row in range(local):
        newer = jnp.where(index == row, age_ref[row], newer)
    stale_rows[...] = jnp.where(
        newer == 1, stale_ref[1].astype(jnp.float32), stale_ref[0].astype(jnp.float32)
    )
    stream_rows[...] = stream_ref[...].astype(jnp.float32)
    for row in range(rows):
        stale = stale_rows[pl.ds(rows_ref[rows + row], 1), :]
        stream = stream_rows[pl.ds(rows_ref[half_ref[0] * rows + row], 1), :]
        for core in range(2):
            keys = stale[:, core * width : (core + 1) * width]
            values = stale[:, (core + 2) * width : (core + 3) * width]
            out_ref[core, row : row + 1, :width] = keys
            out_ref[core, row : row + 1, width:] = values[:, :rest]
            out_ref[core, rows + row : rows + row + 1, : width - rest] = values[:, rest:]
            out_ref[core, rows + row : rows + row + 1, width - rest :] = stream[
                :, core * width : (core + 1) * width
            ]


def offer(ages, patch_rows, upper, stale, stream):
    local, width = stream.shape
    small = pl.BlockSpec(memory_space=pltpu.SMEM)
    return pl.pallas_call(
        offer_kernel,
        out_shape=jax.ShapeDtypeStruct((2, local, 3 * width // 4), jnp.float32),
        in_specs=[small] * 3 + [VMEM] * 2,
        out_specs=VMEM,
        scratch_shapes=[
            pltpu.VMEM((local, 2 * width), jnp.float32),
            pltpu.VMEM((local, width), jnp.float32),
        ],
        compiler_params=PARAMS,
        name="offer",
    )(ages, patch_rows, upper, stale, stream)


def unfold_kernel(taken_ref, kv_ref, x_ref):
    tokens, width = (kv_ref.shape[0] // 2, kv_ref.shape[1])
    rows = 4
    rest = width // 2
    at = lax.broadcasted_iota(jnp.int32, (tokens, 2 * tokens), 0)
    column = lax.broadcasted_iota(jnp.int32, (tokens, 2 * tokens), 1)
    source = at + lax.div(at, rows) * rows
    top = jnp.where(column == source, 1.0, 0.0).astype(jnp.bfloat16)
    bottom = jnp.where(column == source + rows, 1.0, 0.0).astype(jnp.bfloat16)

    def rows_of(matrix, start):
        block = taken_ref[:, start : start + rest]
        return jnp.dot(matrix, block, preferred_element_type=jnp.float32).astype(jnp.bfloat16)

    kv_ref[:tokens, :rest] = rows_of(top, 0)
    kv_ref[:tokens, rest:] = rows_of(top, rest)
    kv_ref[tokens:, :rest] = rows_of(top, width)
    kv_ref[tokens:, rest:] = rows_of(bottom, 0)
    x_ref[:tokens, :rest] = rows_of(bottom, rest)
    x_ref[:tokens, rest:] = rows_of(bottom, width)
    close_stream(x_ref, tokens)


def close_stream(x_ref, tokens):
    width = x_ref.shape[1]
    pieces = [x_ref[:tokens, cut].astype(jnp.float32) for cut in head_slices(width)]
    x_ref[tokens:, :tokens] = half_stats(pieces)
    x_ref[tokens:, tokens:] = jnp.zeros((STAT_ROWS, width - tokens), jnp.bfloat16)


def unfold(taken, width):
    tokens = taken.shape[0] // 2
    return pl.pallas_call(
        unfold_kernel,
        out_shape=(
            jax.ShapeDtypeStruct((2 * tokens, width), jnp.bfloat16),
            jax.ShapeDtypeStruct((tokens + STAT_ROWS, width), jnp.bfloat16),
        ),
        in_specs=[VMEM],
        out_specs=(VMEM,) * 2,
        compiler_params=PARAMS,
        name="unfold",
    )(taken)


def scores(left, right):
    return lax.dot_general(
        left, right, (((1,), (1,)), ((), ())), preferred_element_type=jnp.float32
    )


def unit_norm(part):
    return part * lax.rsqrt(jnp.mean(part * part, axis=1, keepdims=True) + EPS)


def block_kernel(x_ref, st_ref, par_ref, w_ref, other_ref, xo_ref, kv_ref):
    tokens, width = (kv_ref.shape[0] // 2, kv_ref.shape[1])

    def joined(core, first):
        parts = [st_ref[core, first + i : first + i + 1].astype(jnp.float32) for i in range(3)]
        return parts[0] + parts[1] + parts[2]

    mean_a, mean_b = (joined(0, 0), joined(1, 0))
    spread = joined(0, 3) + joined(1, 3) + jnp.square(mean_a - mean_b) * (0.5 * width)
    columns = row_to_columns(
        0.5 * (mean_a + mean_b), lax.rsqrt(spread * (0.5 / width) + EPS)
    )
    mean = jnp.broadcast_to(columns[:, 0:1], (tokens, HEAD_DIM))
    rstd = jnp.broadcast_to(columns[:, 1:2], (tokens, HEAD_DIM))
    query_gain = par_ref[3:4, :HEAD_DIM] * QUERY_SCALE
    key_gain = par_ref[3:4, HEAD_DIM : 2 * HEAD_DIM]
    cuts = head_slices(width)

    def project(head):
        cut = cuts[head]
        x = x_ref[:tokens, cut].astype(jnp.float32)
        mod_in = (x - mean) * rstd * (1.0 + par_ref[1:2, cut]) + par_ref[0:1, cut]
        projected = jnp.dot(
            mod_in.astype(jnp.bfloat16),
            w_ref[head, :, : 3 * HEAD_DIM],
            preferred_element_type=jnp.float32,
        )
        query = (unit_norm(projected[:, :HEAD_DIM]) * query_gain).astype(jnp.bfloat16)
        key = (unit_norm(projected[:, HEAD_DIM : 2 * HEAD_DIM]) * key_gain).astype(jnp.bfloat16)
        value = projected[:, 2 * HEAD_DIM :].astype(jnp.bfloat16)
        kv_ref[:tokens, cut] = key
        kv_ref[tokens:, cut] = value
        return (query, key, value)

    def weigh(head, query, key, value):
        fresh = jnp.exp2(scores(query, key))
        other = jnp.exp2(scores(query, other_ref[:tokens, cuts[head]]))
        total = jnp.sum(fresh + other, axis=1, keepdims=True)
        return (fresh.astype(jnp.bfloat16), other.astype(jnp.bfloat16), total, value)

    def finish(head, fresh, other, total, value):
        cut = cuts[head]
        numerator = jnp.dot(fresh, value, preferred_element_type=jnp.float32) + jnp.dot(
            other, other_ref[tokens:, cut], preferred_element_type=jnp.float32
        )
        branch = jnp.dot(
            (numerator / total).astype(jnp.bfloat16),
            w_ref[head, :, 3 * HEAD_DIM :],
            preferred_element_type=jnp.float32,
        )
        x = x_ref[:tokens, cut].astype(jnp.float32)
        xo_ref[:tokens, cut] = (x + par_ref[2:3, cut] * branch).astype(jnp.bfloat16)

    parts = [project(head) for head in range(len(cuts))]
    ready = weigh(0, *parts[0])
    for head in range(len(cuts)):
        after = weigh(head + 1, *parts[head + 1]) if head + 1 < len(cuts) else None
        finish(head, *ready)
        ready = after
    close_stream(xo_ref, tokens)


def block_step(x, stats, block, other):
    params, weights = block
    width = other.shape[1]
    return pl.pallas_call(
        block_kernel,
        out_shape=(
            jax.ShapeDtypeStruct(x.shape, jnp.bfloat16),
            jax.ShapeDtypeStruct(other.shape, jnp.bfloat16),
        ),
        in_specs=[VMEM] * 5,
        out_specs=(VMEM,) * 2,
        compiler_params=PARAMS,
        cost_estimate=pl.CostEstimate(
            flops=1_000_000, bytes_accessed=100_000, transcendentals=1_000
        ),
        name="block_step",
    )(x, stats, params, weights, other)


def shards(
    stream_in,
    head_maps,
    out_maps,
    norm_gains,
    modulation,
    stale_cache,
    patch_rows,
    stale_age,
    timestep,
):
    local, width = stream_in.shape
    heads = head_maps.shape[1]
    half = width // 2
    rows = local // 2
    span = 2 * rows
    planes, yl_count = (lax.axis_size("x"), lax.axis_size("yl"))
    z_count, seq_count = (lax.axis_size("z"), lax.axis_size(SEQ))
    core, plane, upper = (lax.axis_index("c"), lax.axis_index("x"), lax.axis_index("yh"))
    z, yl = (lax.axis_index("z"), lax.axis_index("yl"))
    tokens = seq_count * rows
    low = yl == 0

    def spot(x, yh, y):
        return (x * 2 + yh) * yl_count + y

    def send(array, pairs):
        return lax.ppermute(array, ("x", "yh", "yl"), pairs)

    last = yl_count - 1
    climb = [(0, last), (last, 0)]

    given = offer(stale_age, patch_rows, upper[None], stale_cache[0], stream_in)
    copies = (seq_count // 2,) + given.shape
    given = jnp.broadcast_to(given.astype(jnp.bfloat16)[None], copies)
    given = given.reshape((seq_count,) + given.shape[2:])
    taken = lax.all_to_all(given, SEQ, split_axis=0, concat_axis=0, tiled=True)

    mod = lax.dynamic_index_in_dim(modulation[0], timestep[0], 0, keepdims=False)
    mod = lax.dynamic_slice_in_dim(mod, core * half, half, axis=1)
    gains = jnp.pad(norm_gains[0].reshape(1, 2 * HEAD_DIM), ((0, 0), (0, half - 2 * HEAD_DIM)))
    params = jnp.concatenate([mod, gains], axis=0)
    weights = jnp.concatenate(
        [
            lax.dynamic_slice_in_dim(head_maps[0], core * (heads // 2), heads // 2),
            lax.dynamic_slice_in_dim(out_maps[0], core * (heads // 2), heads // 2),
        ],
        axis=2,
    )
    own = (params, weights)
    lift = [(spot(x, 0, a), spot(x, 1, b)) for x in range(1, planes) for a, b in climb]
    under_params, taken = lax.optimization_barrier((send(params, lift), taken))
    under = (jnp.where(plane > 0, under_params, params), send(weights, lift))
    kv, x0 = unfold(taken.reshape(seq_count * local, -1), half)
    cross = [(spot(0, 1, b), spot(0, 0, a)) for a, b in climb]
    current = [x0, send(x0, cross)]
    under_kv = send(kv, lift)

    def join(x):
        return lax.all_gather(x[tokens:, :tokens], "c", axis=0)

    def piece(arrays, y):
        at = (z * yl_count + y) * span
        cuts = []
        for fresh, x in arrays:
            cuts += [
                lax.dynamic_slice_in_dim(fresh, at, span),
                lax.dynamic_slice_in_dim(fresh, tokens + at, span),
                lax.dynamic_slice_in_dim(x, at, span),
            ]
        return jnp.stack(cuts)

    beside, far = (jnp.where(low, 1, last - 1), jnp.where(low, last - 1, 1))
    across = jnp.where(low, last, 0)

    found = []
    for step in range(2):
        if step == 0:
            hop = [(spot(0, 0, a), spot(0, 1, b)) for a, b in climb]
        else:
            hop = [(spot(0, 1, y), spot(1, 1, y)) for y in (0, last)]
        done, other = ([], kv)
        for patch in range(2):
            if patch == 1:
                current[1], x = lax.optimization_barrier((current[1], x))
            x, other = block_step(current[patch], join(current[patch]), own, other)
            current[patch] = send(x, hop)
            done.append((other, x))
        found.append((piece(done, yl), piece(done, beside)))
    mine, near = [jnp.where(upper == 0, a, b) for a, b in zip(*found)]

    down = None
    for turn in range(1, planes):
        fresh = [under_kv, kv]
        done = [[], []]
        hop = [(spot(turn, 1, y), spot(turn + 1, 1, y)) for y in (0, last)]
        for patch in range(2):
            if patch == 1:
                current[1], x = lax.optimization_barrier((current[1], x))
            x = current[patch]
            for index, block in enumerate((under, own)):
                x, fresh[index] = block_step(x, join(x), block, fresh[index])
                done[index].append((fresh[index], x))
            if turn < planes - 1:
                current[patch] = send(x, hop)
        here = plane == turn
        new = (piece(done[0], across), piece(done[0], far))
        down = new if down is None else [jnp.where(here, a, b) for a, b in zip(new, down)]
        mine = jnp.where(here, piece(done[1], yl), mine)
        near = jnp.where(here, piece(done[1], beside), near)

    inner = [(0, 1), (last, last - 1)]
    spread = [(spot(x, 1, a), spot(x, 1, b)) for x in range(planes) for a, b in inner]
    spread += [(spot(0, 0, a), spot(0, 0, b)) for a, b in inner]
    descend = [(spot(x, 1, a), spot(x, 0, b)) for x in range(1, planes) for a, b in climb]
    reach = [(0, last - 1), (last, 1)]
    beyond = [(spot(x, 1, a), spot(x, 0, b)) for x in range(1, planes) for a, b in reach]
    got = jnp.where(
        jnp.logical_or(plane == 0, upper == 1),
        send(near, spread),
        jnp.where(jnp.logical_or(low, yl == last), send(down[0], descend), send(down[1], beyond)),
    )
    local_site = jnp.logical_and(
        jnp.logical_or(plane == 0, upper == 1), jnp.logical_or(low, yl == last)
    )
    kept = jnp.where(local_site, mine, got)

    kept = jnp.transpose(kept.reshape(2, 3, 2, rows, half), (2, 0, 1, 3, 4))
    kept = lax.all_to_all(kept, "c", split_axis=0, concat_axis=0, tiled=True)
    kept = jnp.transpose(kept, (1, 3, 2, 0, 4)).reshape(local, 3 * width)
    order = (patch_rows[:, None] == jnp.arange(local)[None, :]).astype(jnp.bfloat16)
    kept = lax.dot_general(order, kept, (((0,), (0,)), ((), ())))
    return (kept[None, :, 2 * width :], kept[None, :, : 2 * width])


def solution(mesh):
    fine = Mesh(mesh.devices.reshape(4, 2, 8, 4, 2), ("x", "yh", "z", "yl", "c"))
    section, seq = (("x", "yh"), SEQ)
    in_specs = (
        P(seq, None),
        P(section, None, None, None),
        P(section, None, None, None),
        P(section, None, None),
        P(section, None, None, None),
        P(section, None, seq, None),
        P(),
        P(seq),
        P(),
    )
    out_specs = (P(section, seq, None), P(section, seq, None))
    return jax.shard_map(shards, mesh=fine, in_specs=in_specs, out_specs=out_specs, check_vma=False)
```

```python
import math

import jax
import jax.numpy as jnp
from jax import lax
from jax.experimental import pallas as pl
from jax.experimental.pallas import tpu as pltpu
from jax.sharding import Mesh
from jax.sharding import PartitionSpec as P

HEAD_DIM = 128
EPS = 1e-06
QUERY_SCALE = HEAD_DIM ** (-0.5) * math.log2(math.e)
VMEM = pl.BlockSpec(memory_space=pltpu.VMEM)
STAT_ROWS = 16
SEQ = ("z", "yl", "c")
PARAMS = pltpu.CompilerParams(vmem_limit_bytes=32 * 2**20)


def row_to_columns(first, second):
    rows = lax.broadcasted_iota(jnp.int32, (HEAD_DIM, first.shape[1]), 0)
    return jnp.transpose(jnp.where(rows == 0, first, second))


def split_rows(row):
    parts = []
    for _ in range(3):
        part = row.astype(jnp.bfloat16).astype(jnp.float32)
        parts.append(part)
        row = row - part
    return parts


def half_stats(pieces):
    width = len(pieces) * HEAD_DIM
    total = pieces[0]
    for piece in pieces[1:]:
        total = total + piece
    center = jnp.sum(total, axis=1, keepdims=True) * (1.0 / width)
    squares = jnp.square(pieces[0] - center)
    for piece in pieces[1:]:
        squares = squares + jnp.square(piece - center)
    spread = jnp.sum(squares, axis=1, keepdims=True)
    lanes = lax.broadcasted_iota(jnp.int32, squares.shape, 1)
    both = jnp.transpose(jnp.where(lanes == 0, center, spread))
    rows = lax.broadcasted_iota(jnp.int32, (STAT_ROWS, both.shape[1]), 0)
    packed = jnp.zeros(rows.shape, jnp.float32)
    for index, part in enumerate(split_rows(both[0:1]) + split_rows(both[1:2])):
        packed = jnp.where(rows == index, part, packed)
    return packed.astype(jnp.bfloat16)


def head_slices(width):
    return [slice(h * HEAD_DIM, (h + 1) * HEAD_DIM) for h in range(width // HEAD_DIM)]


def offer_kernel(
    half_ref, age_hbm, rows_hbm, stale_hbm, stream_hbm, out_ref,
    age_ref, rows_ref, stale_ref, stream_ref, stale_rows, stream_rows, sems,
):
    pairs = (
        (age_hbm, age_ref),
        (rows_hbm, rows_ref),
        (stale_hbm, stale_ref),
        (stream_hbm, stream_ref),
    )
    copies = [
        pltpu.make_async_copy(source, target, sems.at[i])
        for i, (source, target) in enumerate(pairs)
    ]
    for copy in copies:
        copy.start()
    for copy in copies:
        copy.wait()
    local = stream_ref.shape[0]
    rows = local // 2
    width = stream_ref.shape[1] // 2
    fold = 3 * width // 2
    rest = fold - width
    index = lax.broadcasted_iota(jnp.int32, (local, 1), 0)
    newer = jnp.zeros((local, 1), jnp.int32)
    for row in range(local):
        newer = jnp.where(index == row, age_ref[row], newer)
    stale_rows[...] = jnp.where(
        newer == 1, stale_ref[1].astype(jnp.float32), stale_ref[0].astype(jnp.float32)
    )
    stream_rows[...] = stream_ref[...].astype(jnp.float32)
    for row in range(rows):
        stale = stale_rows[pl.ds(rows_ref[rows + row], 1), :]
        stream = stream_rows[pl.ds(rows_ref[half_ref[0] * rows + row], 1), :]
        for core in range(2):
            keys = stale[:, core * width : (core + 1) * width]
            values = stale[:, (core + 2) * width : (core + 3) * width]
            out_ref[core, row : row + 1, :width] = keys
            out_ref[core, row : row + 1, width:] = values[:, :rest]
            out_ref[core, rows + row : rows + row + 1, : width - rest] = values[:, rest:]
            out_ref[core, rows + row : rows + row + 1, width - rest :] = stream[
                :, core * width : (core + 1) * width
            ]


def offer(patch, ages, patch_rows, stale, stream):
    local, width = stream.shape
    small = pl.BlockSpec(memory_space=pltpu.SMEM)
    return pl.pallas_call(
        offer_kernel,
        out_shape=jax.ShapeDtypeStruct((2, local, 3 * width // 4), jnp.float32),
        in_specs=[small] + [pl.BlockSpec(memory_space=pltpu.HBM)] * 4,
        out_specs=VMEM,
        scratch_shapes=[
            pltpu.SMEM(ages.shape, jnp.int32),
            pltpu.SMEM(patch_rows.shape, jnp.int32),
            pltpu.VMEM(stale.shape, stale.dtype),
            pltpu.VMEM(stream.shape, stream.dtype),
            pltpu.VMEM((local, 2 * width), jnp.float32),
            pltpu.VMEM((local, width), jnp.float32),
            pltpu.SemaphoreType.DMA((4,)),
        ],
        compiler_params=PARAMS,
        name="offer",
    )(patch, ages, patch_rows, stale, stream)


def unfold_kernel(taken_ref, kv_ref, x_ref):
    tokens, width = (kv_ref.shape[0] // 2, kv_ref.shape[1])
    rows = 4
    rest = width // 2
    at = lax.broadcasted_iota(jnp.int32, (tokens, 2 * tokens), 0)
    column = lax.broadcasted_iota(jnp.int32, (tokens, 2 * tokens), 1)
    source = at + lax.div(at, rows) * rows
    top = jnp.where(column == source, 1.0, 0.0).astype(jnp.bfloat16)
    bottom = jnp.where(column == source + rows, 1.0, 0.0).astype(jnp.bfloat16)

    def rows_of(matrix, start):
        block = taken_ref[:, start : start + rest]
        return jnp.dot(matrix, block, preferred_element_type=jnp.float32).astype(jnp.bfloat16)

    kv_ref[:tokens, :rest] = rows_of(top, 0)
    kv_ref[:tokens, rest:] = rows_of(top, rest)
    kv_ref[tokens:, :rest] = rows_of(top, width)
    kv_ref[tokens:, rest:] = rows_of(bottom, 0)
    x_ref[:tokens, :rest] = rows_of(bottom, rest)
    x_ref[:tokens, rest:] = rows_of(bottom, width)
    close_stream(x_ref, tokens)


def close_stream(x_ref, tokens):
    width = x_ref.shape[1]
    pieces = [x_ref[:tokens, cut].astype(jnp.float32) for cut in head_slices(width)]
    x_ref[tokens:, :tokens] = half_stats(pieces)
    x_ref[tokens:, tokens:] = jnp.zeros((STAT_ROWS, width - tokens), jnp.bfloat16)


def unfold(taken, width):
    tokens = taken.shape[0] // 2
    return pl.pallas_call(
        unfold_kernel,
        out_shape=(
            jax.ShapeDtypeStruct((2 * tokens, width), jnp.bfloat16),
            jax.ShapeDtypeStruct((tokens + STAT_ROWS, width), jnp.bfloat16),
        ),
        in_specs=[VMEM],
        out_specs=(VMEM,) * 2,
        compiler_params=PARAMS,
        name="unfold",
    )(taken)


def scores(left, right):
    return lax.dot_general(
        left, right, (((1,), (1,)), ((), ())), preferred_element_type=jnp.float32
    )


def unit_norm(part):
    return part * lax.rsqrt(jnp.mean(part * part, axis=1, keepdims=True) + EPS)


def block_kernel(x_ref, st_ref, par_ref, w_ref, other_ref, xo_ref, kv_ref):
    tokens, width = (kv_ref.shape[0] // 2, kv_ref.shape[1])

    def joined(core, first):
        parts = [st_ref[core, first + i : first + i + 1].astype(jnp.float32) for i in range(3)]
        return parts[0] + parts[1] + parts[2]

    mean_a, mean_b = (joined(0, 0), joined(1, 0))
    spread = joined(0, 3) + joined(1, 3) + jnp.square(mean_a - mean_b) * (0.5 * width)
    columns = row_to_columns(
        0.5 * (mean_a + mean_b), lax.rsqrt(spread * (0.5 / width) + EPS)
    )
    mean = jnp.broadcast_to(columns[:, 0:1], (tokens, HEAD_DIM))
    rstd = jnp.broadcast_to(columns[:, 1:2], (tokens, HEAD_DIM))
    query_gain = par_ref[3:4, :HEAD_DIM] * QUERY_SCALE
    key_gain = par_ref[3:4, HEAD_DIM : 2 * HEAD_DIM]
    cuts = head_slices(width)

    def project(head):
        cut = cuts[head]
        x = x_ref[:tokens, cut].astype(jnp.float32)
        mod_in = (x - mean) * rstd * (1.0 + par_ref[1:2, cut]) + par_ref[0:1, cut]
        projected = jnp.dot(
            mod_in.astype(jnp.bfloat16),
            w_ref[head, :, : 3 * HEAD_DIM],
            preferred_element_type=jnp.float32,
        )
        query = (unit_norm(projected[:, :HEAD_DIM]) * query_gain).astype(jnp.bfloat16)
        key = (unit_norm(projected[:, HEAD_DIM : 2 * HEAD_DIM]) * key_gain).astype(jnp.bfloat16)
        value = projected[:, 2 * HEAD_DIM :].astype(jnp.bfloat16)
        kv_ref[:tokens, cut] = key
        kv_ref[tokens:, cut] = value
        return (query, key, value)

    def weigh(head, query, key, value):
        fresh = jnp.exp2(scores(query, key))
        other = jnp.exp2(scores(query, other_ref[:tokens, cuts[head]]))
        total = jnp.sum(fresh + other, axis=1, keepdims=True)
        return (fresh.astype(jnp.bfloat16), other.astype(jnp.bfloat16), total, value)

    def finish(head, fresh, other, total, value):
        cut = cuts[head]
        numerator = jnp.dot(fresh, value, preferred_element_type=jnp.float32) + jnp.dot(
            other, other_ref[tokens:, cut], preferred_element_type=jnp.float32
        )
        branch = jnp.dot(
            (numerator / total).astype(jnp.bfloat16),
            w_ref[head, :, 3 * HEAD_DIM :],
            preferred_element_type=jnp.float32,
        )
        x = x_ref[:tokens, cut].astype(jnp.float32)
        xo_ref[:tokens, cut] = (x + par_ref[2:3, cut] * branch).astype(jnp.bfloat16)

    parts = [project(head) for head in range(len(cuts))]
    ready = weigh(0, *parts[0])
    for head in range(len(cuts)):
        after = weigh(head + 1, *parts[head + 1]) if head + 1 < len(cuts) else None
        finish(head, *ready)
        ready = after
    close_stream(xo_ref, tokens)


def block_step(x, stats, block, other):
    params, weights = block
    width = other.shape[1]
    return pl.pallas_call(
        block_kernel,
        out_shape=(
            jax.ShapeDtypeStruct(x.shape, jnp.bfloat16),
            jax.ShapeDtypeStruct(other.shape, jnp.bfloat16),
        ),
        in_specs=[VMEM] * 5,
        out_specs=(VMEM,) * 2,
        compiler_params=PARAMS,
        cost_estimate=pl.CostEstimate(
            flops=1_000_000, bytes_accessed=100_000, transcendentals=1_000
        ),
        name="block_step",
    )(x, stats, params, weights, other)


def shards(
    stream_in,
    head_maps,
    out_maps,
    norm_gains,
    modulation,
    stale_cache,
    patch_rows,
    stale_age,
    timestep,
):
    local, width = stream_in.shape
    heads = head_maps.shape[1]
    half = width // 2
    rows = local // 2
    span = 2 * rows
    planes, yl_count = (lax.axis_size("x"), lax.axis_size("yl"))
    z_count, seq_count = (lax.axis_size("z"), lax.axis_size(SEQ))
    core, plane, upper = (lax.axis_index("c"), lax.axis_index("x"), lax.axis_index("yh"))
    z, yl = (lax.axis_index("z"), lax.axis_index("yl"))
    tokens = seq_count * rows
    low = yl == 0

    def spot(x, yh, y):
        return (x * 2 + yh) * yl_count + y

    def send(array, pairs):
        return lax.ppermute(array, ("x", "yh", "yl"), pairs)

    last = yl_count - 1
    climb = [(0, last), (last, 0)]

    patch = jnp.where(plane == 0, 0, 1).astype(jnp.int32)
    given = offer(patch[None], stale_age, patch_rows, stale_cache[0], stream_in)
    copies = (seq_count // 2,) + given.shape
    given = jnp.broadcast_to(given.astype(jnp.bfloat16)[None], copies)
    given = given.reshape((seq_count,) + given.shape[2:])
    taken = lax.all_to_all(given, SEQ, split_axis=0, concat_axis=0, tiled=True)

    mod = lax.dynamic_index_in_dim(modulation[0], timestep[0], 0, keepdims=False)
    mod = lax.dynamic_slice_in_dim(mod, core * half, half, axis=1)
    gains = jnp.pad(norm_gains[0].reshape(1, 2 * HEAD_DIM), ((0, 0), (0, half - 2 * HEAD_DIM)))
    params = jnp.concatenate([mod, gains], axis=0)
    weights = jnp.concatenate(
        [
            lax.dynamic_slice_in_dim(head_maps[0], core * (heads // 2), heads // 2),
            lax.dynamic_slice_in_dim(out_maps[0], core * (heads // 2), heads // 2),
        ],
        axis=2,
    )
    own = (params, weights)
    lift = [(spot(x, 0, a), spot(x, 1, b)) for x in range(1, planes) for a, b in climb]
    under_params, taken = lax.optimization_barrier((send(params, lift), taken))
    under = (jnp.where(plane > 0, under_params, params), send(weights, lift))
    kv, x0 = unfold(taken.reshape(seq_count * local, -1), half)
    under_kv = send(kv, lift)

    def tail(x):
        return x[tokens:, :tokens]

    def join(x):
        return lax.all_gather(tail(x), "c", axis=0)

    def hop(x, pairs):
        arrived = send(x, pairs)
        swapped = [(2 * a + i, 2 * b + 1 - i) for a, b in pairs for i in range(2)]
        partner = lax.ppermute(tail(x), ("x", "yh", "yl", "c"), swapped)
        return (arrived, jnp.stack([tail(arrived), partner]))

    across_planes = [(spot(1, 0, y), spot(0, 0, y)) for y in (0, last)]
    current = [(x0, join(x0)), (send(x0, across_planes), None)]

    def piece(arrays, y):
        at = (z * yl_count + y) * span
        cuts = []
        for fresh, x in arrays:
            cuts += [
                lax.dynamic_slice_in_dim(fresh, at, span),
                lax.dynamic_slice_in_dim(fresh, tokens + at, span),
                lax.dynamic_slice_in_dim(x, at, span),
            ]
        return jnp.stack(cuts)

    beside, far = (jnp.where(low, 1, last - 1), jnp.where(low, last - 1, 1))
    across = jnp.where(low, last, 0)

    found = []
    for step in range(2):
        if step == 0:
            way = [(spot(0, 0, a), spot(0, 1, b)) for a, b in climb]
        else:
            way = [(spot(0, 1, y), spot(1, 1, y)) for y in (0, last)]
        done, other = ([], kv)
        for patch in range(2):
            came, stat = current[patch]
            if step or patch:
                came, x = lax.optimization_barrier((came, x))
            stat = join(came) if stat is None else stat
            x, other = block_step(came, stat, own, other)
            current[patch] = (send(x, way), None) if step or patch else hop(x, way)
            done.append((other, x))
        found.append((piece(done, yl), piece(done, beside)))
    mine, near = [jnp.where(upper == 0, a, b) for a, b in zip(*found)]

    down = None
    for turn in range(1, planes):
        fresh = [under_kv, kv]
        done = [[], []]
        way = [(spot(turn, 1, y), spot(turn + 1, 1, y)) for y in (0, last)]
        for patch in range(2):
            came, x = lax.optimization_barrier((current[patch][0], x))
            x = came
            for index, block in enumerate((under, own)):
                x, fresh[index] = block_step(x, join(x), block, fresh[index])
                done[index].append((fresh[index], x))
            if turn < planes - 1:
                current[patch] = (send(x, way), None)
        here = plane == turn
        new = (piece(done[0], across), piece(done[0], far))
        down = new if down is None else [jnp.where(here, a, b) for a, b in zip(new, down)]
        mine = jnp.where(here, piece(done[1], yl), mine)
        near = jnp.where(here, piece(done[1], beside), near)

    inner = [(0, 1), (last, last - 1)]
    spread = [(spot(x, 1, a), spot(x, 1, b)) for x in range(planes) for a, b in inner]
    spread += [(spot(0, 0, a), spot(0, 0, b)) for a, b in inner]
    descend = [(spot(x, 1, a), spot(x, 0, b)) for x in range(1, planes) for a, b in climb]
    reach = [(0, last - 1), (last, 1)]
    beyond = [(spot(x, 1, a), spot(x, 0, b)) for x in range(1, planes) for a, b in reach]
    got = jnp.where(
        jnp.logical_or(plane == 0, upper == 1),
        send(near, spread),
        jnp.where(jnp.logical_or(low, yl == last), send(down[0], descend), send(down[1], beyond)),
    )
    local_site = jnp.logical_and(
        jnp.logical_or(plane == 0, upper == 1), jnp.logical_or(low, yl == last)
    )
    kept = jnp.where(local_site, mine, got)

    kept = lax.all_gather(kept, "c", axis=0).reshape(2, 2, 3, 2, rows, half)
    kept = lax.dynamic_index_in_dim(kept, core, 3, keepdims=False)
    kept = jnp.transpose(kept, (1, 3, 2, 0, 4)).reshape(local, 3 * width)
    order = (patch_rows[:, None] == jnp.arange(local)[None, :]).astype(jnp.bfloat16)
    kept = lax.dot_general(order, kept, (((0,), (0,)), ((), ())))
    return (kept[None, :, 2 * width :], kept[None, :, : 2 * width])


def solution(mesh):
    fine = Mesh(mesh.devices.reshape(4, 2, 8, 4, 2), ("x", "yh", "z", "yl", "c"))
    section, seq = (("x", "yh"), SEQ)
    in_specs = (
        P(seq, None),
        P(section, None, None, None),
        P(section, None, None, None),
        P(section, None, None),
        P(section, None, None, None),
        P(section, None, seq, None),
        P(),
        P(seq),
        P(),
    )
    out_specs = (P(section, seq, None), P(section, seq, None))
    return jax.shard_map(shards, mesh=fine, in_specs=in_specs, out_specs=out_specs, check_vma=False)
```

```python
import math

import jax
import jax.numpy as jnp
from jax import lax
from jax.experimental import pallas as pl
from jax.experimental.pallas import tpu as pltpu
from jax.sharding import Mesh
from jax.sharding import PartitionSpec as P

HEAD_DIM = 128
EPS = 1e-06
QUERY_SCALE = HEAD_DIM ** (-0.5) * math.log2(math.e)
VMEM = pl.BlockSpec(memory_space=pltpu.VMEM)
STAT_ROWS = 16
SEQ = ("z", "yl", "c")
PARAMS = pltpu.CompilerParams(vmem_limit_bytes=32 * 2**20)


def row_to_columns(first, second):
    rows = lax.broadcasted_iota(jnp.int32, (HEAD_DIM, first.shape[1]), 0)
    return jnp.transpose(jnp.where(rows == 0, first, second))


def split_rows(row):
    parts = []
    for _ in range(3):
        part = row.astype(jnp.bfloat16).astype(jnp.float32)
        parts.append(part)
        row = row - part
    return parts


def half_stats(pieces):
    width = len(pieces) * HEAD_DIM
    total = pieces[0]
    for piece in pieces[1:]:
        total = total + piece
    center = jnp.sum(total, axis=1, keepdims=True) * (1.0 / width)
    squares = jnp.square(pieces[0] - center)
    for piece in pieces[1:]:
        squares = squares + jnp.square(piece - center)
    spread = jnp.sum(squares, axis=1, keepdims=True)
    lanes = lax.broadcasted_iota(jnp.int32, squares.shape, 1)
    both = jnp.transpose(jnp.where(lanes == 0, center, spread))
    rows = lax.broadcasted_iota(jnp.int32, (STAT_ROWS, both.shape[1]), 0)
    packed = jnp.zeros(rows.shape, jnp.float32)
    for index, part in enumerate(split_rows(both[0:1]) + split_rows(both[1:2])):
        packed = jnp.where(rows == index, part, packed)
    return packed.astype(jnp.bfloat16)


def head_slices(width):
    return [slice(h * HEAD_DIM, (h + 1) * HEAD_DIM) for h in range(width // HEAD_DIM)]


def offer_kernel(
    half_ref, age_hbm, rows_hbm, stale_hbm, stream_hbm, copies_hbm,
    age_ref, rows_ref, stale_ref, stream_ref, stale_rows, stream_rows, out_ref, piece_ref, sems,
    copy_sems,
):
    pairs = (
        (age_hbm, age_ref),
        (rows_hbm, rows_ref),
        (stale_hbm, stale_ref),
        (stream_hbm, stream_ref),
    )
    copies = [
        pltpu.make_async_copy(source, target, sems.at[i])
        for i, (source, target) in enumerate(pairs)
    ]
    for copy in copies:
        copy.start()
    for copy in copies:
        copy.wait()
    local = stream_ref.shape[0]
    rows = local // 2
    width = stream_ref.shape[1] // 2
    fold = 3 * width // 2
    rest = fold - width
    index = lax.broadcasted_iota(jnp.int32, (local, 1), 0)
    newer = jnp.zeros((local, 1), jnp.int32)
    for row in range(local):
        newer = jnp.where(index == row, age_ref[row], newer)
    stale_rows[...] = jnp.where(
        newer == 1, stale_ref[1].astype(jnp.float32), stale_ref[0].astype(jnp.float32)
    )
    stream_rows[...] = stream_ref[...].astype(jnp.float32)
    for row in range(rows):
        stale = stale_rows[pl.ds(rows_ref[rows + row], 1), :]
        stream = stream_rows[pl.ds(rows_ref[half_ref[0] * rows + row], 1), :]
        for core in range(2):
            keys = stale[:, core * width : (core + 1) * width]
            values = stale[:, (core + 2) * width : (core + 3) * width]
            out_ref[core, row : row + 1, :width] = keys
            out_ref[core, row : row + 1, width:] = values[:, :rest]
            out_ref[core, rows + row : rows + row + 1, : width - rest] = values[:, rest:]
            out_ref[core, rows + row : rows + row + 1, width - rest :] = stream[
                :, core * width : (core + 1) * width
            ]
    for core in range(2):
        piece_ref[core] = out_ref[core].astype(jnp.bfloat16)
    copies = [
        pltpu.make_async_copy(piece_ref, copies_hbm.at[pl.ds(2 * i, 2)], copy_sems.at[i])
        for i in range(copies_hbm.shape[0] // 2)
    ]
    for copy in copies:
        copy.start()
    for copy in copies:
        copy.wait()


def offer(patch, ages, patch_rows, stale, stream, count):
    local, width = stream.shape
    small = pl.BlockSpec(memory_space=pltpu.SMEM)
    return pl.pallas_call(
        offer_kernel,
        out_shape=jax.ShapeDtypeStruct((count, local, 3 * width // 4), jnp.bfloat16),
        in_specs=[small] + [pl.BlockSpec(memory_space=pltpu.HBM)] * 4,
        out_specs=pl.BlockSpec(memory_space=pltpu.HBM),
        scratch_shapes=[
            pltpu.SMEM(ages.shape, jnp.int32),
            pltpu.SMEM(patch_rows.shape, jnp.int32),
            pltpu.VMEM(stale.shape, stale.dtype),
            pltpu.VMEM(stream.shape, stream.dtype),
            pltpu.VMEM((local, 2 * width), jnp.float32),
            pltpu.VMEM((local, width), jnp.float32),
            pltpu.VMEM((2, local, 3 * width // 4), jnp.float32),
            pltpu.VMEM((2, local, 3 * width // 4), jnp.bfloat16),
            pltpu.SemaphoreType.DMA((4,)),
            pltpu.SemaphoreType.DMA((count // 2,)),
        ],
        compiler_params=pltpu.CompilerParams(vmem_limit_bytes=60 * 2**20),
        name="offer",
    )(patch, ages, patch_rows, stale, stream)


def unfold_kernel(taken_ref, kv_ref, x_ref):
    tokens, width = (kv_ref.shape[0] // 2, kv_ref.shape[1])
    rows, block = (4, 128)
    rest, part = (width // 2, block // 2)
    at = lax.broadcasted_iota(jnp.int32, (block, block), 0)
    column = lax.broadcasted_iota(jnp.int32, (block, block), 1)
    upper = lax.div(at, part)
    token = at - upper * part
    source = token + lax.div(token, rows) * rows + upper * rows
    pick = jnp.where(column == source, 1.0, 0.0).astype(jnp.bfloat16)
    for index in range(taken_ref.shape[0] // block):
        piece = taken_ref[index * block : (index + 1) * block, :]
        moved = jnp.dot(pick, piece, preferred_element_type=jnp.float32).astype(jnp.bfloat16)
        top, bottom = (moved[:part], moved[part:])
        first = slice(index * part, (index + 1) * part)
        second = slice(tokens + index * part, tokens + (index + 1) * part)
        kv_ref[first, :] = top[:, :width]
        kv_ref[second, :rest] = top[:, width:]
        kv_ref[second, rest:] = bottom[:, :rest]
        x_ref[first, :] = bottom[:, rest:]
    close_stream(x_ref, tokens)


def close_stream(x_ref, tokens):
    width = x_ref.shape[1]
    pieces = [x_ref[:tokens, cut].astype(jnp.float32) for cut in head_slices(width)]
    x_ref[tokens:, :tokens] = half_stats(pieces)
    x_ref[tokens:, tokens:] = jnp.zeros((STAT_ROWS, width - tokens), jnp.bfloat16)


def unfold(taken, width):
    tokens = taken.shape[0] // 2
    return pl.pallas_call(
        unfold_kernel,
        out_shape=(
            jax.ShapeDtypeStruct((2 * tokens, width), jnp.bfloat16),
            jax.ShapeDtypeStruct((tokens + STAT_ROWS, width), jnp.bfloat16),
        ),
        in_specs=[VMEM],
        out_specs=(VMEM,) * 2,
        compiler_params=PARAMS,
        name="unfold",
    )(taken)


def scores(left, right):
    return lax.dot_general(
        left, right, (((1,), (1,)), ((), ())), preferred_element_type=jnp.float32
    )


def unit_norm(part):
    return part * lax.rsqrt(jnp.mean(part * part, axis=1, keepdims=True) + EPS)


def settle_kernel(core_ref, rows_ref, both_ref, block_ref, fresh_ref, rows_in, rows_out):
    count, span, half = both_ref.shape
    rows = span // 2
    kinds = count // 4
    for index in range(count):
        rows_in[index] = both_ref[index].astype(jnp.float32)
    for patch in range(2):
        for row in range(rows):
            source = core_ref[0] * rows + row
            target = rows_ref[patch * rows + row]
            for core in range(2):
                for kind in range(kinds):
                    at = (kind * 2 + core) * half
                    index = (core * 2 + patch) * kinds + kind
                    rows_out[pl.ds(target, 1), at : at + half] = rows_in[
                        index, pl.ds(source, 1), :
                    ]
    cut = 4 * half
    fresh_ref[...] = rows_out[:, :cut].astype(jnp.bfloat16)
    block_ref[...] = rows_out[:, cut:].astype(jnp.bfloat16)


def settle(core, patch_rows, both):
    count, span, half = both.shape
    small = pl.BlockSpec(memory_space=pltpu.SMEM)
    return pl.pallas_call(
        settle_kernel,
        out_shape=(
            jax.ShapeDtypeStruct((span, 2 * half), jnp.bfloat16),
            jax.ShapeDtypeStruct((span, 4 * half), jnp.bfloat16),
        ),
        in_specs=[small] * 2 + [VMEM],
        out_specs=(VMEM,) * 2,
        scratch_shapes=[
            pltpu.VMEM(both.shape, jnp.float32),
            pltpu.VMEM((span, 6 * half), jnp.float32),
        ],
        compiler_params=PARAMS,
        name="settle",
    )(core, patch_rows, both)


def block_kernel(x_ref, st_ref, par_ref, w_ref, other_ref, xo_ref, kv_ref):
    tokens, width = (kv_ref.shape[0] // 2, kv_ref.shape[1])

    def joined(core, first):
        parts = [st_ref[core, first + i : first + i + 1].astype(jnp.float32) for i in range(3)]
        return parts[0] + parts[1] + parts[2]

    mean_a, mean_b = (joined(0, 0), joined(1, 0))
    spread = joined(0, 3) + joined(1, 3) + jnp.square(mean_a - mean_b) * (0.5 * width)
    columns = row_to_columns(
        0.5 * (mean_a + mean_b), lax.rsqrt(spread * (0.5 / width) + EPS)
    )
    mean = jnp.broadcast_to(columns[:, 0:1], (tokens, HEAD_DIM))
    rstd = jnp.broadcast_to(columns[:, 1:2], (tokens, HEAD_DIM))
    query_gain = par_ref[3:4, :HEAD_DIM] * QUERY_SCALE
    key_gain = par_ref[3:4, HEAD_DIM : 2 * HEAD_DIM]
    cuts = head_slices(width)

    def project(head):
        cut = cuts[head]
        x = x_ref[:tokens, cut].astype(jnp.float32)
        mod_in = (x - mean) * rstd * (1.0 + par_ref[1:2, cut]) + par_ref[0:1, cut]
        projected = jnp.dot(
            mod_in.astype(jnp.bfloat16),
            w_ref[head, :, : 3 * HEAD_DIM],
            preferred_element_type=jnp.float32,
        )
        query = (unit_norm(projected[:, :HEAD_DIM]) * query_gain).astype(jnp.bfloat16)
        key = (unit_norm(projected[:, HEAD_DIM : 2 * HEAD_DIM]) * key_gain).astype(jnp.bfloat16)
        value = projected[:, 2 * HEAD_DIM :].astype(jnp.bfloat16)
        kv_ref[:tokens, cut] = key
        kv_ref[tokens:, cut] = value
        return (query, key, value)

    def weigh(head, query, key, value):
        fresh = jnp.exp2(scores(query, key))
        other = jnp.exp2(scores(query, other_ref[:tokens, cuts[head]]))
        total = jnp.sum(fresh + other, axis=1, keepdims=True)
        return (fresh.astype(jnp.bfloat16), other.astype(jnp.bfloat16), total, value)

    def finish(head, fresh, other, total, value):
        cut = cuts[head]
        numerator = jnp.dot(fresh, value, preferred_element_type=jnp.float32) + jnp.dot(
            other, other_ref[tokens:, cut], preferred_element_type=jnp.float32
        )
        branch = jnp.dot(
            (numerator / total).astype(jnp.bfloat16),
            w_ref[head, :, 3 * HEAD_DIM :],
            preferred_element_type=jnp.float32,
        )
        x = x_ref[:tokens, cut].astype(jnp.float32)
        xo_ref[:tokens, cut] = (x + par_ref[2:3, cut] * branch).astype(jnp.bfloat16)

    parts = [project(head) for head in range(len(cuts))]
    ready = weigh(0, *parts[0])
    for head in range(len(cuts)):
        after = weigh(head + 1, *parts[head + 1]) if head + 1 < len(cuts) else None
        finish(head, *ready)
        ready = after
    close_stream(xo_ref, tokens)


def block_step(x, stats, block, other):
    params, weights = block
    width = other.shape[1]
    return pl.pallas_call(
        block_kernel,
        out_shape=(
            jax.ShapeDtypeStruct(x.shape, jnp.bfloat16),
            jax.ShapeDtypeStruct(other.shape, jnp.bfloat16),
        ),
        in_specs=[VMEM] * 5,
        out_specs=(VMEM,) * 2,
        compiler_params=PARAMS,
        cost_estimate=pl.CostEstimate(
            flops=1_000_000, bytes_accessed=100_000, transcendentals=1_000
        ),
        name="block_step",
    )(x, stats, params, weights, other)


def shards(
    stream_in,
    head_maps,
    out_maps,
    norm_gains,
    modulation,
    stale_cache,
    patch_rows,
    stale_age,
    timestep,
):
    local, width = stream_in.shape
    heads = head_maps.shape[1]
    half = width // 2
    rows = local // 2
    span = 2 * rows
    planes, yl_count = (lax.axis_size("x"), lax.axis_size("yl"))
    z_count, seq_count = (lax.axis_size("z"), lax.axis_size(SEQ))
    core, plane, upper = (lax.axis_index("c"), lax.axis_index("x"), lax.axis_index("yh"))
    z, yl = (lax.axis_index("z"), lax.axis_index("yl"))
    tokens = seq_count * rows
    low = yl == 0

    def spot(x, yh, y):
        return (x * 2 + yh) * yl_count + y

    def send(array, pairs):
        return lax.ppermute(array, ("x", "yh", "yl"), pairs)

    last = yl_count - 1
    climb = [(0, last), (last, 0)]

    patch = jnp.where(plane == 0, 0, 1).astype(jnp.int32)
    given = offer(patch[None], stale_age, patch_rows, stale_cache[0], stream_in, seq_count)
    taken = lax.all_to_all(given, SEQ, split_axis=0, concat_axis=0, tiled=True)

    mod = lax.dynamic_index_in_dim(modulation[0], timestep[0], 0, keepdims=False)
    mod = lax.dynamic_slice_in_dim(mod, core * half, half, axis=1)
    gains = jnp.pad(norm_gains[0].reshape(1, 2 * HEAD_DIM), ((0, 0), (0, half - 2 * HEAD_DIM)))
    params = jnp.concatenate([mod, gains], axis=0)
    weights = jnp.concatenate(
        [
            lax.dynamic_slice_in_dim(head_maps[0], core * (heads // 2), heads // 2),
            lax.dynamic_slice_in_dim(out_maps[0], core * (heads // 2), heads // 2),
        ],
        axis=2,
    )
    own = (params, weights)
    lift = [(spot(x, 0, a), spot(x, 1, b)) for x in range(1, planes) for a, b in climb]
    under_params, taken = lax.optimization_barrier((send(params, lift), taken))
    under = (jnp.where(plane > 0, under_params, params), send(weights, lift))
    kv, x0 = unfold(taken.reshape(seq_count * local, -1), half)

    def tail(x):
        return x[tokens:, :tokens]

    def join(x):
        return lax.all_gather(tail(x), "c", axis=0)

    def hop(x, pairs):
        arrived = send(x, pairs)
        swapped = [(2 * a + i, 2 * b + 1 - i) for a, b in pairs for i in range(2)]
        partner = lax.ppermute(tail(x), ("x", "yh", "yl", "c"), swapped)
        return (arrived, jnp.stack([tail(arrived), partner]))

    across_planes = [(spot(1, 0, y), spot(0, 0, y)) for y in (0, last)]
    current = [(x0, join(x0)), None]

    def piece(arrays, y):
        at = (z * yl_count + y) * span
        cuts = []
        for fresh, x in arrays:
            cuts += [
                lax.dynamic_slice_in_dim(fresh, at, span),
                lax.dynamic_slice_in_dim(fresh, tokens + at, span),
                lax.dynamic_slice_in_dim(x, at, span),
            ]
        return jnp.stack(cuts)

    beside, far = (jnp.where(low, 1, last - 1), jnp.where(low, last - 1, 1))
    across = jnp.where(low, last, 0)

    found = []
    for step in range(2):
        if step == 0:
            way = [(spot(0, 0, a), spot(0, 1, b)) for a, b in climb]
        else:
            way = [(spot(0, 1, y), spot(1, 1, y)) for y in (0, last)]
        done, other = ([], kv)
        for patch in range(2):
            came, stat = current[patch]
            if step or patch:
                came, x = lax.optimization_barrier((came, x))
            stat = join(came) if stat is None else stat
            x, other = block_step(came, stat, own, other)
            if step or patch:
                current[patch] = (send(x, way), None)
            else:
                current[0] = hop(x, way)
                crossing, lifted, _ = lax.optimization_barrier((x0, kv, x))
                current[1] = (send(crossing, across_planes), None)
                under_kv = send(lifted, lift)
            done.append((other, x))
        found.append((piece(done, yl), piece(done, beside)))
    mine, near = [jnp.where(upper == 0, a, b) for a, b in zip(*found)]

    down = None
    for turn in range(1, planes):
        fresh = [under_kv, kv]
        done = [[], []]
        way = [(spot(turn, 1, y), spot(turn + 1, 1, y)) for y in (0, last)]
        for patch in range(2):
            came, x = lax.optimization_barrier((current[patch][0], x))
            x = came
            for index, block in enumerate((under, own)):
                x, fresh[index] = block_step(x, join(x), block, fresh[index])
                done[index].append((fresh[index], x))
            if turn < planes - 1:
                current[patch] = (send(x, way), None)
        here = plane == turn
        new = (piece(done[0], across), piece(done[0], far))
        down = new if down is None else [jnp.where(here, a, b) for a, b in zip(new, down)]
        mine = jnp.where(here, piece(done[1], yl), mine)
        near = jnp.where(here, piece(done[1], beside), near)

    inner = [(0, 1), (last, last - 1)]
    spread = [(spot(x, 1, a), spot(x, 1, b)) for x in range(planes) for a, b in inner]
    spread += [(spot(0, 0, a), spot(0, 0, b)) for a, b in inner]
    descend = [(spot(x, 1, a), spot(x, 0, b)) for x in range(1, planes) for a, b in climb]
    reach = [(0, last - 1), (last, 1)]
    beyond = [(spot(x, 1, a), spot(x, 0, b)) for x in range(1, planes) for a, b in reach]
    got = jnp.where(
        jnp.logical_or(plane == 0, upper == 1),
        send(near, spread),
        jnp.where(jnp.logical_or(low, yl == last), send(down[0], descend), send(down[1], beyond)),
    )
    local_site = jnp.logical_and(
        jnp.logical_or(plane == 0, upper == 1), jnp.logical_or(low, yl == last)
    )
    kept = jnp.where(local_site, mine, got)

    both = lax.all_gather(kept, "c", axis=0).reshape((-1,) + kept.shape[1:])
    block_out, fresh_out = settle(core[None].astype(jnp.int32), patch_rows, both)
    return (block_out[None], fresh_out[None])


def solution(mesh):
    fine = Mesh(mesh.devices.reshape(4, 2, 8, 4, 2), ("x", "yh", "z", "yl", "c"))
    section, seq = (("x", "yh"), SEQ)
    in_specs = (
        P(seq, None),
        P(section, None, None, None),
        P(section, None, None, None),
        P(section, None, None),
        P(section, None, None, None),
        P(section, None, seq, None),
        P(),
        P(seq),
        P(),
    )
    out_specs = (P(section, seq, None), P(section, seq, None))
    return jax.shard_map(shards, mesh=fine, in_specs=in_specs, out_specs=out_specs, check_vma=False)
```

```python
import functools
import math

import jax
import jax.numpy as jnp
from jax import lax
from jax.experimental import pallas as pl
from jax.experimental.pallas import tpu as pltpu
from jax.sharding import Mesh
from jax.sharding import PartitionSpec as P

HEAD_DIM = 128
EPS = 1e-06
QUERY_SCALE = HEAD_DIM ** (-0.5) * math.log2(math.e)
VMEM = pl.BlockSpec(memory_space=pltpu.VMEM)
STAT_ROWS = 16
SEQ = ("z", "yl", "c")
PARAMS = pltpu.CompilerParams(vmem_limit_bytes=32 * 2**20)


def row_to_columns(first, second):
    rows = lax.broadcasted_iota(jnp.int32, (HEAD_DIM, first.shape[1]), 0)
    return jnp.transpose(jnp.where(rows == 0, first, second))


def split_rows(row):
    parts = []
    for _ in range(3):
        part = row.astype(jnp.bfloat16).astype(jnp.float32)
        parts.append(part)
        row = row - part
    return parts


def half_stats(pieces):
    width = len(pieces) * HEAD_DIM
    total = pieces[0]
    for piece in pieces[1:]:
        total = total + piece
    center = jnp.sum(total, axis=1, keepdims=True) * (1.0 / width)
    squares = jnp.square(pieces[0] - center)
    for piece in pieces[1:]:
        squares = squares + jnp.square(piece - center)
    spread = jnp.sum(squares, axis=1, keepdims=True)
    lanes = lax.broadcasted_iota(jnp.int32, squares.shape, 1)
    both = jnp.transpose(jnp.where(lanes == 0, center, spread))
    rows = lax.broadcasted_iota(jnp.int32, (STAT_ROWS, both.shape[1]), 0)
    packed = jnp.zeros(rows.shape, jnp.float32)
    for index, part in enumerate(split_rows(both[0:1]) + split_rows(both[1:2])):
        packed = jnp.where(rows == index, part, packed)
    return packed.astype(jnp.bfloat16)


def head_slices(width):
    return [slice(h * HEAD_DIM, (h + 1) * HEAD_DIM) for h in range(width // HEAD_DIM)]


def offer_kernel(
    half_ref, age_hbm, rows_hbm, stale_hbm, stream_hbm, copies_hbm,
    age_ref, rows_ref, stale_ref, stream_ref, stale_rows, stream_rows, out_ref, piece_ref, sems,
    copy_sems,
):
    pairs = (
        (age_hbm, age_ref),
        (rows_hbm, rows_ref),
        (stale_hbm, stale_ref),
        (stream_hbm, stream_ref),
    )
    copies = [
        pltpu.make_async_copy(source, target, sems.at[i])
        for i, (source, target) in enumerate(pairs)
    ]
    for copy in copies:
        copy.start()
    for copy in copies:
        copy.wait()
    local = stream_ref.shape[0]
    rows = local // 2
    width = stream_ref.shape[1] // 2
    fold = 3 * width // 2
    rest = fold - width
    index = lax.broadcasted_iota(jnp.int32, (local, 1), 0)
    newer = jnp.zeros((local, 1), jnp.int32)
    for row in range(local):
        newer = jnp.where(index == row, age_ref[row], newer)
    stale_rows[...] = jnp.where(
        newer == 1, stale_ref[1].astype(jnp.float32), stale_ref[0].astype(jnp.float32)
    )
    stream_rows[...] = stream_ref[...].astype(jnp.float32)
    for row in range(rows):
        stale = stale_rows[pl.ds(rows_ref[rows + row], 1), :]
        stream = stream_rows[pl.ds(rows_ref[half_ref[0] * rows + row], 1), :]
        for core in range(2):
            keys = stale[:, core * width : (core + 1) * width]
            values = stale[:, (core + 2) * width : (core + 3) * width]
            out_ref[core, row : row + 1, :width] = keys
            out_ref[core, row : row + 1, width:] = values[:, :rest]
            out_ref[core, rows + row : rows + row + 1, : width - rest] = values[:, rest:]
            out_ref[core, rows + row : rows + row + 1, width - rest :] = stream[
                :, core * width : (core + 1) * width
            ]
    for core in range(2):
        piece_ref[core] = out_ref[core].astype(jnp.bfloat16)
    copies = [
        pltpu.make_async_copy(piece_ref, copies_hbm.at[pl.ds(2 * i, 2)], copy_sems.at[i])
        for i in range(copies_hbm.shape[0] // 2)
    ]
    for copy in copies:
        copy.start()
    for copy in copies:
        copy.wait()


def offer(patch, ages, patch_rows, stale, stream, count):
    local, width = stream.shape
    small = pl.BlockSpec(memory_space=pltpu.SMEM)
    return pl.pallas_call(
        offer_kernel,
        out_shape=jax.ShapeDtypeStruct((count, local, 3 * width // 4), jnp.bfloat16),
        in_specs=[small] + [pl.BlockSpec(memory_space=pltpu.HBM)] * 4,
        out_specs=pl.BlockSpec(memory_space=pltpu.HBM),
        scratch_shapes=[
            pltpu.SMEM(ages.shape, jnp.int32),
            pltpu.SMEM(patch_rows.shape, jnp.int32),
            pltpu.VMEM(stale.shape, stale.dtype),
            pltpu.VMEM(stream.shape, stream.dtype),
            pltpu.VMEM((local, 2 * width), jnp.float32),
            pltpu.VMEM((local, width), jnp.float32),
            pltpu.VMEM((2, local, 3 * width // 4), jnp.float32),
            pltpu.VMEM((2, local, 3 * width // 4), jnp.bfloat16),
            pltpu.SemaphoreType.DMA((4,)),
            pltpu.SemaphoreType.DMA((count // 2,)),
        ],
        compiler_params=pltpu.CompilerParams(vmem_limit_bytes=60 * 2**20),
        name="offer",
    )(patch, ages, patch_rows, stale, stream)


def unfold_kernel(taken_ref, kv_ref, x_ref):
    tokens, width = (kv_ref.shape[0] // 2, kv_ref.shape[1])
    rows, block = (4, 128)
    rest, part = (width // 2, block // 2)
    at = lax.broadcasted_iota(jnp.int32, (block, block), 0)
    column = lax.broadcasted_iota(jnp.int32, (block, block), 1)
    upper = lax.div(at, part)
    token = at - upper * part
    source = token + lax.div(token, rows) * rows + upper * rows
    pick = jnp.where(column == source, 1.0, 0.0).astype(jnp.bfloat16)
    for index in range(taken_ref.shape[0] // block):
        piece = taken_ref[index * block : (index + 1) * block, :]
        moved = jnp.dot(pick, piece, preferred_element_type=jnp.float32).astype(jnp.bfloat16)
        top, bottom = (moved[:part], moved[part:])
        first = slice(index * part, (index + 1) * part)
        second = slice(tokens + index * part, tokens + (index + 1) * part)
        kv_ref[first, :] = top[:, :width]
        kv_ref[second, :rest] = top[:, width:]
        kv_ref[second, rest:] = bottom[:, :rest]
        x_ref[first, :] = bottom[:, rest:]
    close_stream(x_ref, tokens)


def close_stream(x_ref, tokens):
    width = x_ref.shape[1]
    pieces = [x_ref[:tokens, cut].astype(jnp.float32) for cut in head_slices(width)]
    x_ref[tokens:, :tokens] = half_stats(pieces)
    x_ref[tokens:, tokens:] = jnp.zeros((STAT_ROWS, width - tokens), jnp.bfloat16)


def unfold(taken, width):
    tokens = taken.shape[0] // 2
    return pl.pallas_call(
        unfold_kernel,
        out_shape=(
            jax.ShapeDtypeStruct((2 * tokens, width), jnp.bfloat16),
            jax.ShapeDtypeStruct((tokens + STAT_ROWS, width), jnp.bfloat16),
        ),
        in_specs=[VMEM],
        out_specs=(VMEM,) * 2,
        compiler_params=PARAMS,
        name="unfold",
    )(taken)


def scores(left, right):
    return lax.dot_general(
        left, right, (((1,), (1,)), ((), ())), preferred_element_type=jnp.float32
    )


def unit_norm(part):
    return part * lax.rsqrt(jnp.mean(part * part, axis=1, keepdims=True) + EPS)


def settle_kernel(core_ref, rows_ref, both_ref, block_ref, fresh_ref, rows_in, rows_out):
    count, span, half = both_ref.shape
    rows = span // 2
    kinds = count // 4
    for index in range(count):
        rows_in[index] = both_ref[index].astype(jnp.float32)
    for patch in range(2):
        for row in range(rows):
            source = core_ref[0] * rows + row
            target = rows_ref[patch * rows + row]
            for core in range(2):
                for kind in range(kinds):
                    at = (kind * 2 + core) * half
                    index = (core * 2 + patch) * kinds + kind
                    rows_out[pl.ds(target, 1), at : at + half] = rows_in[
                        index, pl.ds(source, 1), :
                    ]
    cut = 4 * half
    fresh_ref[...] = rows_out[:, :cut].astype(jnp.bfloat16)
    block_ref[...] = rows_out[:, cut:].astype(jnp.bfloat16)


def settle(core, patch_rows, both):
    count, span, half = both.shape
    small = pl.BlockSpec(memory_space=pltpu.SMEM)
    return pl.pallas_call(
        settle_kernel,
        out_shape=(
            jax.ShapeDtypeStruct((span, 2 * half), jnp.bfloat16),
            jax.ShapeDtypeStruct((span, 4 * half), jnp.bfloat16),
        ),
        in_specs=[small] * 2 + [VMEM],
        out_specs=(VMEM,) * 2,
        scratch_shapes=[
            pltpu.VMEM(both.shape, jnp.float32),
            pltpu.VMEM((span, 6 * half), jnp.float32),
        ],
        compiler_params=PARAMS,
        name="settle",
    )(core, patch_rows, both)


def block_kernel(site, *refs):
    here = jnp.logical_and(lax.axis_index("x") == site[0], lax.axis_index("yh") == site[1])
    pl.when(here)(lambda: compute_block(*refs))


def compute_block(x_ref, st_ref, par_ref, w_ref, other_ref, xo_ref, kv_ref):
    tokens, width = (kv_ref.shape[0] // 2, kv_ref.shape[1])

    def joined(core, first):
        parts = [st_ref[core, first + i : first + i + 1].astype(jnp.float32) for i in range(3)]
        return parts[0] + parts[1] + parts[2]

    mean_a, mean_b = (joined(0, 0), joined(1, 0))
    spread = joined(0, 3) + joined(1, 3) + jnp.square(mean_a - mean_b) * (0.5 * width)
    columns = row_to_columns(
        0.5 * (mean_a + mean_b), lax.rsqrt(spread * (0.5 / width) + EPS)
    )
    mean = jnp.broadcast_to(columns[:, 0:1], (tokens, HEAD_DIM))
    rstd = jnp.broadcast_to(columns[:, 1:2], (tokens, HEAD_DIM))
    query_gain = par_ref[3:4, :HEAD_DIM] * QUERY_SCALE
    key_gain = par_ref[3:4, HEAD_DIM : 2 * HEAD_DIM]
    cuts = head_slices(width)

    def project(head):
        cut = cuts[head]
        x = x_ref[:tokens, cut].astype(jnp.float32)
        mod_in = (x - mean) * rstd * (1.0 + par_ref[1:2, cut]) + par_ref[0:1, cut]
        projected = jnp.dot(
            mod_in.astype(jnp.bfloat16),
            w_ref[head, :, : 3 * HEAD_DIM],
            preferred_element_type=jnp.float32,
        )
        query = (unit_norm(projected[:, :HEAD_DIM]) * query_gain).astype(jnp.bfloat16)
        key = (unit_norm(projected[:, HEAD_DIM : 2 * HEAD_DIM]) * key_gain).astype(jnp.bfloat16)
        value = projected[:, 2 * HEAD_DIM :].astype(jnp.bfloat16)
        kv_ref[:tokens, cut] = key
        kv_ref[tokens:, cut] = value
        return (query, key, value)

    def weigh(head, query, key, value):
        fresh = jnp.exp2(scores(query, key))
        other = jnp.exp2(scores(query, other_ref[:tokens, cuts[head]]))
        total = jnp.sum(fresh + other, axis=1, keepdims=True)
        return (fresh.astype(jnp.bfloat16), other.astype(jnp.bfloat16), total, value)

    def finish(head, fresh, other, total, value):
        cut = cuts[head]
        numerator = jnp.dot(fresh, value, preferred_element_type=jnp.float32) + jnp.dot(
            other, other_ref[tokens:, cut], preferred_element_type=jnp.float32
        )
        branch = jnp.dot(
            (numerator / total).astype(jnp.bfloat16),
            w_ref[head, :, 3 * HEAD_DIM :],
            preferred_element_type=jnp.float32,
        )
        x = x_ref[:tokens, cut].astype(jnp.float32)
        xo_ref[:tokens, cut] = (x + par_ref[2:3, cut] * branch).astype(jnp.bfloat16)

    parts = [project(head) for head in range(len(cuts))]
    ready = weigh(0, *parts[0])
    for head in range(len(cuts)):
        after = weigh(head + 1, *parts[head + 1]) if head + 1 < len(cuts) else None
        finish(head, *ready)
        ready = after
    close_stream(xo_ref, tokens)


def block_step(site, x, stats, block, other):
    params, weights = block
    return pl.pallas_call(
        functools.partial(block_kernel, site),
        out_shape=(
            jax.ShapeDtypeStruct(x.shape, jnp.bfloat16),
            jax.ShapeDtypeStruct(other.shape, jnp.bfloat16),
        ),
        in_specs=[VMEM] * 5,
        out_specs=(VMEM,) * 2,
        compiler_params=PARAMS,
        cost_estimate=pl.CostEstimate(
            flops=1_000_000, bytes_accessed=100_000, transcendentals=1_000
        ),
        name="block_step",
    )(x, stats, params, weights, other)


def shards(
    stream_in,
    head_maps,
    out_maps,
    norm_gains,
    modulation,
    stale_cache,
    patch_rows,
    stale_age,
    timestep,
):
    local, width = stream_in.shape
    heads = head_maps.shape[1]
    half = width // 2
    rows = local // 2
    span = 2 * rows
    planes, yl_count = (lax.axis_size("x"), lax.axis_size("yl"))
    z_count, seq_count = (lax.axis_size("z"), lax.axis_size(SEQ))
    core, plane, upper = (lax.axis_index("c"), lax.axis_index("x"), lax.axis_index("yh"))
    z, yl = (lax.axis_index("z"), lax.axis_index("yl"))
    tokens = seq_count * rows
    low = yl == 0

    def spot(x, yh, y):
        return (x * 2 + yh) * yl_count + y

    def send(array, pairs):
        return lax.ppermute(array, ("x", "yh", "yl"), pairs)

    last = yl_count - 1
    climb = [(0, last), (last, 0)]

    patch = jnp.where(plane == 0, 0, 1).astype(jnp.int32)
    given = offer(patch[None], stale_age, patch_rows, stale_cache[0], stream_in, seq_count)
    taken = lax.all_to_all(given, SEQ, split_axis=0, concat_axis=0, tiled=True)

    mod = lax.dynamic_index_in_dim(modulation[0], timestep[0], 0, keepdims=False)
    mod = lax.dynamic_slice_in_dim(mod, core * half, half, axis=1)
    gains = jnp.pad(norm_gains[0].reshape(1, 2 * HEAD_DIM), ((0, 0), (0, half - 2 * HEAD_DIM)))
    params = jnp.concatenate([mod, gains], axis=0)
    weights = jnp.concatenate(
        [
            lax.dynamic_slice_in_dim(head_maps[0], core * (heads // 2), heads // 2),
            lax.dynamic_slice_in_dim(out_maps[0], core * (heads // 2), heads // 2),
        ],
        axis=2,
    )
    own = (params, weights)
    lift = [(spot(x, 0, a), spot(x, 1, b)) for x in range(1, planes) for a, b in climb]
    under_params, taken = lax.optimization_barrier((send(params, lift), taken))
    under = (jnp.where(plane > 0, under_params, params), send(weights, lift))
    kv, x0 = unfold(taken.reshape(seq_count * local, -1), half)

    def tail(x):
        return x[tokens:, :tokens]

    def join(x):
        return lax.all_gather(tail(x), "c", axis=0)

    def hop(x, pairs):
        arrived = send(x, pairs)
        swapped = [(2 * a + i, 2 * b + 1 - i) for a, b in pairs for i in range(2)]
        partner = lax.ppermute(tail(x), ("x", "yh", "yl", "c"), swapped)
        return (arrived, jnp.stack([tail(arrived), partner]))

    across_planes = [(spot(1, 0, y), spot(0, 0, y)) for y in (0, last)]
    current = [(x0, join(x0)), (send(x0, across_planes), None)]

    def piece(arrays, y):
        at = (z * yl_count + y) * span
        cuts = []
        for fresh, x in arrays:
            cuts += [
                lax.dynamic_slice_in_dim(fresh, at, span),
                lax.dynamic_slice_in_dim(fresh, tokens + at, span),
                lax.dynamic_slice_in_dim(x, at, span),
            ]
        return jnp.stack(cuts)

    beside, far = (jnp.where(low, 1, last - 1), jnp.where(low, last - 1, 1))
    across = jnp.where(low, last, 0)

    found = []
    for step in range(2):
        if step == 0:
            way = [(spot(0, 0, a), spot(0, 1, b)) for a, b in climb]
        else:
            way = [(spot(0, 1, y), spot(1, 1, y)) for y in (0, last)]
        done, other = ([], kv)
        for patch in range(2):
            came, stat = current[patch]
            if step or patch:
                came, x = lax.optimization_barrier((came, x))
            stat = join(came) if stat is None else stat
            x, other = block_step((0, step), came, stat, own, other)
            if step or patch:
                current[patch] = (send(x, way), None)
            else:
                current[0] = hop(x, way)
                lifted, _ = lax.optimization_barrier((kv, x))
                under_kv = send(lifted, lift)
            done.append((other, x))
        found.append((piece(done, yl), piece(done, beside)))
    mine, near = [jnp.where(upper == 0, a, b) for a, b in zip(*found)]

    down = None
    for turn in range(1, planes):
        fresh = [under_kv, kv]
        done = [[], []]
        way = [(spot(turn, 1, y), spot(turn + 1, 1, y)) for y in (0, last)]
        for patch in range(2):
            came, x = lax.optimization_barrier((current[patch][0], x))
            x = came
            for index, block in enumerate((under, own)):
                x, fresh[index] = block_step((turn, 1), x, join(x), block, fresh[index])
                done[index].append((fresh[index], x))
            if turn < planes - 1:
                current[patch] = (send(x, way), None)
        here = plane == turn
        new = (piece(done[0], across), piece(done[0], far))
        down = new if down is None else [jnp.where(here, a, b) for a, b in zip(new, down)]
        mine = jnp.where(here, piece(done[1], yl), mine)
        near = jnp.where(here, piece(done[1], beside), near)

    inner = [(0, 1), (last, last - 1)]
    spread = [(spot(x, 1, a), spot(x, 1, b)) for x in range(planes) for a, b in inner]
    spread += [(spot(0, 0, a), spot(0, 0, b)) for a, b in inner]
    descend = [(spot(x, 1, a), spot(x, 0, b)) for x in range(1, planes) for a, b in climb]
    reach = [(0, last - 1), (last, 1)]
    beyond = [(spot(x, 1, a), spot(x, 0, b)) for x in range(1, planes) for a, b in reach]
    got = jnp.where(
        jnp.logical_or(plane == 0, upper == 1),
        send(near, spread),
        jnp.where(jnp.logical_or(low, yl == last), send(down[0], descend), send(down[1], beyond)),
    )
    local_site = jnp.logical_and(
        jnp.logical_or(plane == 0, upper == 1), jnp.logical_or(low, yl == last)
    )
    kept = jnp.where(local_site, mine, got)

    both = lax.all_gather(kept, "c", axis=0).reshape((-1,) + kept.shape[1:])
    block_out, fresh_out = settle(core[None].astype(jnp.int32), patch_rows, both)
    return (block_out[None], fresh_out[None])


def solution(mesh):
    fine = Mesh(mesh.devices.reshape(4, 2, 8, 4, 2), ("x", "yh", "z", "yl", "c"))
    section, seq = (("x", "yh"), SEQ)
    in_specs = (
        P(seq, None),
        P(section, None, None, None),
        P(section, None, None, None),
        P(section, None, None),
        P(section, None, None, None),
        P(section, None, seq, None),
        P(),
        P(seq),
        P(),
    )
    out_specs = (P(section, seq, None), P(section, seq, None))
    return jax.shard_map(shards, mesh=fine, in_specs=in_specs, out_specs=out_specs, check_vma=False)
```

```python
import functools
import math

import jax
import jax.numpy as jnp
from jax import lax
from jax.experimental import pallas as pl
from jax.experimental.pallas import tpu as pltpu
from jax.sharding import Mesh
from jax.sharding import PartitionSpec as P

HEAD_DIM = 128
EPS = 1e-06
QUERY_SCALE = HEAD_DIM ** (-0.5) * math.log2(math.e)
VMEM = pl.BlockSpec(memory_space=pltpu.VMEM)
STAT_ROWS = 16
SEQ = ("z", "yl", "c")
PARAMS = pltpu.CompilerParams(vmem_limit_bytes=32 * 2**20)


def row_to_columns(first, second):
    rows = lax.broadcasted_iota(jnp.int32, (HEAD_DIM, first.shape[1]), 0)
    return jnp.transpose(jnp.where(rows == 0, first, second))


def split_rows(row):
    parts = []
    for _ in range(3):
        part = row.astype(jnp.bfloat16).astype(jnp.float32)
        parts.append(part)
        row = row - part
    return parts


def half_stats(pieces):
    width = len(pieces) * HEAD_DIM
    total = pieces[0]
    for piece in pieces[1:]:
        total = total + piece
    center = jnp.sum(total, axis=1, keepdims=True) * (1.0 / width)
    squares = jnp.square(pieces[0] - center)
    for piece in pieces[1:]:
        squares = squares + jnp.square(piece - center)
    spread = jnp.sum(squares, axis=1, keepdims=True)
    lanes = lax.broadcasted_iota(jnp.int32, squares.shape, 1)
    both = jnp.transpose(jnp.where(lanes == 0, center, spread))
    rows = lax.broadcasted_iota(jnp.int32, (STAT_ROWS, both.shape[1]), 0)
    packed = jnp.zeros(rows.shape, jnp.float32)
    for index, part in enumerate(split_rows(both[0:1]) + split_rows(both[1:2])):
        packed = jnp.where(rows == index, part, packed)
    return packed.astype(jnp.bfloat16)


def head_slices(width):
    return [slice(h * HEAD_DIM, (h + 1) * HEAD_DIM) for h in range(width // HEAD_DIM)]


def offer_kernel(
    half_ref, age_hbm, rows_hbm, stale_hbm, stream_hbm, copies_hbm,
    age_ref, rows_ref, stale_ref, stream_ref, stale_rows, stream_rows, out_ref, piece_ref, sems,
    copy_sems,
):
    pairs = (
        (age_hbm, age_ref),
        (rows_hbm, rows_ref),
        (stale_hbm, stale_ref),
        (stream_hbm, stream_ref),
    )
    copies = [
        pltpu.make_async_copy(source, target, sems.at[i])
        for i, (source, target) in enumerate(pairs)
    ]
    for copy in copies:
        copy.start()
    for copy in copies:
        copy.wait()
    local = stream_ref.shape[0]
    rows = local // 2
    width = stream_ref.shape[1] // 2
    fold = 3 * width // 2
    rest = fold - width
    index = lax.broadcasted_iota(jnp.int32, (local, 1), 0)
    newer = jnp.zeros((local, 1), jnp.int32)
    for row in range(local):
        newer = jnp.where(index == row, age_ref[row], newer)
    stale_rows[...] = jnp.where(
        newer == 1, stale_ref[1].astype(jnp.float32), stale_ref[0].astype(jnp.float32)
    )
    stream_rows[...] = stream_ref[...].astype(jnp.float32)
    for row in range(rows):
        stale = stale_rows[pl.ds(rows_ref[rows + row], 1), :]
        stream = stream_rows[pl.ds(rows_ref[half_ref[0] * rows + row], 1), :]
        for core in range(2):
            keys = stale[:, core * width : (core + 1) * width]
            values = stale[:, (core + 2) * width : (core + 3) * width]
            out_ref[core, row : row + 1, :width] = keys
            out_ref[core, row : row + 1, width:] = values[:, :rest]
            out_ref[core, rows + row : rows + row + 1, : width - rest] = values[:, rest:]
            out_ref[core, rows + row : rows + row + 1, width - rest :] = stream[
                :, core * width : (core + 1) * width
            ]
    for core in range(2):
        piece_ref[core] = out_ref[core].astype(jnp.bfloat16)
    copies = [
        pltpu.make_async_copy(piece_ref, copies_hbm.at[pl.ds(2 * i, 2)], copy_sems.at[i])
        for i in range(copies_hbm.shape[0] // 2)
    ]
    for copy in copies:
        copy.start()
    for copy in copies:
        copy.wait()


def offer(patch, ages, patch_rows, stale, stream, count):
    local, width = stream.shape
    small = pl.BlockSpec(memory_space=pltpu.SMEM)
    return pl.pallas_call(
        offer_kernel,
        out_shape=jax.ShapeDtypeStruct((count, local, 3 * width // 4), jnp.bfloat16),
        in_specs=[small] + [pl.BlockSpec(memory_space=pltpu.HBM)] * 4,
        out_specs=pl.BlockSpec(memory_space=pltpu.HBM),
        scratch_shapes=[
            pltpu.SMEM(ages.shape, jnp.int32),
            pltpu.SMEM(patch_rows.shape, jnp.int32),
            pltpu.VMEM(stale.shape, stale.dtype),
            pltpu.VMEM(stream.shape, stream.dtype),
            pltpu.VMEM((local, 2 * width), jnp.float32),
            pltpu.VMEM((local, width), jnp.float32),
            pltpu.VMEM((2, local, 3 * width // 4), jnp.float32),
            pltpu.VMEM((2, local, 3 * width // 4), jnp.bfloat16),
            pltpu.SemaphoreType.DMA((4,)),
            pltpu.SemaphoreType.DMA((count // 2,)),
        ],
        compiler_params=pltpu.CompilerParams(vmem_limit_bytes=60 * 2**20),
        name="offer",
    )(patch, ages, patch_rows, stale, stream)


def unfold_kernel(taken_ref, kv_ref, x_ref):
    tokens, width = (kv_ref.shape[0] // 2, kv_ref.shape[1])
    rows, block = (4, 128)
    rest, part = (width // 2, block // 2)
    at = lax.broadcasted_iota(jnp.int32, (block, block), 0)
    column = lax.broadcasted_iota(jnp.int32, (block, block), 1)
    upper = lax.div(at, part)
    token = at - upper * part
    source = token + lax.div(token, rows) * rows + upper * rows
    pick = jnp.where(column == source, 1.0, 0.0).astype(jnp.bfloat16)
    for index in range(taken_ref.shape[0] // block):
        piece = taken_ref[index * block : (index + 1) * block, :]
        moved = jnp.dot(pick, piece, preferred_element_type=jnp.float32).astype(jnp.bfloat16)
        top, bottom = (moved[:part], moved[part:])
        first = slice(index * part, (index + 1) * part)
        second = slice(tokens + index * part, tokens + (index + 1) * part)
        kv_ref[first, :] = top[:, :width]
        kv_ref[second, :rest] = top[:, width:]
        kv_ref[second, rest:] = bottom[:, :rest]
        x_ref[first, :] = bottom[:, rest:]
    close_stream(x_ref, tokens)


def close_stream(x_ref, tokens):
    width = x_ref.shape[1]
    pieces = [x_ref[:tokens, cut].astype(jnp.float32) for cut in head_slices(width)]
    x_ref[tokens:, :tokens] = half_stats(pieces)
    x_ref[tokens:, tokens:] = jnp.zeros((STAT_ROWS, width - tokens), jnp.bfloat16)


def unfold(taken, width):
    tokens = taken.shape[0] // 2
    return pl.pallas_call(
        unfold_kernel,
        out_shape=(
            jax.ShapeDtypeStruct((2 * tokens, width), jnp.bfloat16),
            jax.ShapeDtypeStruct((tokens + STAT_ROWS, width), jnp.bfloat16),
        ),
        in_specs=[VMEM],
        out_specs=(VMEM,) * 2,
        compiler_params=PARAMS,
        name="unfold",
    )(taken)


def scores(left, right):
    return lax.dot_general(
        left, right, (((1,), (1,)), ((), ())), preferred_element_type=jnp.float32
    )


def unit_norm(part):
    return part * lax.rsqrt(jnp.mean(part * part, axis=1, keepdims=True) + EPS)


def settle_kernel(core_ref, rows_ref, both_ref, block_ref, fresh_ref, rows_in, rows_out):
    count, span, half = both_ref.shape
    rows = span // 2
    kinds = count // 4
    for index in range(count):
        rows_in[index] = both_ref[index].astype(jnp.float32)
    for patch in range(2):
        for row in range(rows):
            source = core_ref[0] * rows + row
            target = rows_ref[patch * rows + row]
            for core in range(2):
                for kind in range(kinds):
                    at = (kind * 2 + core) * half
                    index = (core * 2 + patch) * kinds + kind
                    rows_out[pl.ds(target, 1), at : at + half] = rows_in[
                        index, pl.ds(source, 1), :
                    ]
    cut = 4 * half
    fresh_ref[...] = rows_out[:, :cut].astype(jnp.bfloat16)
    block_ref[...] = rows_out[:, cut:].astype(jnp.bfloat16)


def settle(core, patch_rows, both):
    count, span, half = both.shape
    small = pl.BlockSpec(memory_space=pltpu.SMEM)
    return pl.pallas_call(
        settle_kernel,
        out_shape=(
            jax.ShapeDtypeStruct((span, 2 * half), jnp.bfloat16),
            jax.ShapeDtypeStruct((span, 4 * half), jnp.bfloat16),
        ),
        in_specs=[small] * 2 + [VMEM],
        out_specs=(VMEM,) * 2,
        scratch_shapes=[
            pltpu.VMEM(both.shape, jnp.float32),
            pltpu.VMEM((span, 6 * half), jnp.float32),
        ],
        compiler_params=PARAMS,
        name="settle",
    )(core, patch_rows, both)


def block_kernel(site, *refs):
    here = jnp.logical_and(lax.axis_index("x") == site[0], lax.axis_index("yh") == site[1])
    pl.when(here)(lambda: compute_block(*refs))


def compute_block(x_ref, st_ref, par_ref, w_ref, other_ref, xo_ref, kv_ref):
    tokens, width = (kv_ref.shape[0] // 2, kv_ref.shape[1])

    def joined(core, first):
        parts = [st_ref[core, first + i : first + i + 1].astype(jnp.float32) for i in range(3)]
        return parts[0] + parts[1] + parts[2]

    mean_a, mean_b = (joined(0, 0), joined(1, 0))
    spread = joined(0, 3) + joined(1, 3) + jnp.square(mean_a - mean_b) * (0.5 * width)
    columns = row_to_columns(
        0.5 * (mean_a + mean_b), lax.rsqrt(spread * (0.5 / width) + EPS)
    )
    mean = jnp.broadcast_to(columns[:, 0:1], (tokens, HEAD_DIM))
    rstd = jnp.broadcast_to(columns[:, 1:2], (tokens, HEAD_DIM))
    query_gain = par_ref[3:4, :HEAD_DIM] * QUERY_SCALE
    key_gain = par_ref[3:4, HEAD_DIM : 2 * HEAD_DIM]
    cuts = head_slices(width)

    def project(head):
        cut = cuts[head]
        x = x_ref[:tokens, cut].astype(jnp.float32)
        mod_in = (x - mean) * rstd * (1.0 + par_ref[1:2, cut]) + par_ref[0:1, cut]
        projected = jnp.dot(
            mod_in.astype(jnp.bfloat16),
            w_ref[head, :, : 3 * HEAD_DIM],
            preferred_element_type=jnp.float32,
        )
        query = (unit_norm(projected[:, :HEAD_DIM]) * query_gain).astype(jnp.bfloat16)
        key = (unit_norm(projected[:, HEAD_DIM : 2 * HEAD_DIM]) * key_gain).astype(jnp.bfloat16)
        value = projected[:, 2 * HEAD_DIM :].astype(jnp.bfloat16)
        kv_ref[:tokens, cut] = key
        kv_ref[tokens:, cut] = value
        return (query, key, value)

    def weigh(head, query, key, value):
        fresh = jnp.exp2(scores(query, key))
        other = jnp.exp2(scores(query, other_ref[:tokens, cuts[head]]))
        total = jnp.sum(fresh + other, axis=1, keepdims=True)
        return (fresh.astype(jnp.bfloat16), other.astype(jnp.bfloat16), total, value)

    def finish(head, fresh, other, total, value):
        cut = cuts[head]
        numerator = jnp.dot(fresh, value, preferred_element_type=jnp.float32) + jnp.dot(
            other, other_ref[tokens:, cut], preferred_element_type=jnp.float32
        )
        branch = jnp.dot(
            (numerator / total).astype(jnp.bfloat16),
            w_ref[head, :, 3 * HEAD_DIM :],
            preferred_element_type=jnp.float32,
        )
        x = x_ref[:tokens, cut].astype(jnp.float32)
        xo_ref[:tokens, cut] = (x + par_ref[2:3, cut] * branch).astype(jnp.bfloat16)

    parts = [project(head) for head in range(len(cuts))]
    ready = weigh(0, *parts[0])
    for head in range(len(cuts)):
        after = weigh(head + 1, *parts[head + 1]) if head + 1 < len(cuts) else None
        finish(head, *ready)
        ready = after
    close_stream(xo_ref, tokens)


def block_step(site, x, stats, block, other):
    params, weights = block
    return pl.pallas_call(
        functools.partial(block_kernel, site),
        out_shape=(
            jax.ShapeDtypeStruct(x.shape, jnp.bfloat16),
            jax.ShapeDtypeStruct(other.shape, jnp.bfloat16),
        ),
        in_specs=[VMEM] * 5,
        out_specs=(VMEM,) * 2,
        compiler_params=PARAMS,
        cost_estimate=pl.CostEstimate(
            flops=1_000_000, bytes_accessed=100_000, transcendentals=1_000
        ),
        name="block_step",
    )(x, stats, params, weights, other)


def shards(
    stream_in,
    head_maps,
    out_maps,
    norm_gains,
    modulation,
    stale_cache,
    patch_rows,
    stale_age,
    timestep,
):
    local, width = stream_in.shape
    heads = head_maps.shape[1]
    half = width // 2
    rows = local // 2
    span = 2 * rows
    planes, yl_count = (lax.axis_size("x"), lax.axis_size("yl"))
    z_count, seq_count = (lax.axis_size("z"), lax.axis_size(SEQ))
    core, plane, upper = (lax.axis_index("c"), lax.axis_index("x"), lax.axis_index("yh"))
    z, yl = (lax.axis_index("z"), lax.axis_index("yl"))
    tokens = seq_count * rows
    low = yl == 0

    def spot(x, yh, y):
        return (x * 2 + yh) * yl_count + y

    def send(array, pairs):
        return lax.ppermute(array, ("x", "yh", "yl"), pairs)

    last = yl_count - 1
    climb = [(0, last), (last, 0)]

    patch = jnp.where(plane == 0, 0, 1).astype(jnp.int32)
    given = offer(patch[None], stale_age, patch_rows, stale_cache[0], stream_in, seq_count)
    taken = lax.all_to_all(given, SEQ, split_axis=0, concat_axis=0, tiled=True)

    mod = lax.dynamic_index_in_dim(modulation[0], timestep[0], 0, keepdims=False)
    mod = lax.dynamic_slice_in_dim(mod, core * half, half, axis=1)
    gains = jnp.pad(norm_gains[0].reshape(1, 2 * HEAD_DIM), ((0, 0), (0, half - 2 * HEAD_DIM)))
    params = jnp.concatenate([mod, gains], axis=0)
    weights = jnp.concatenate(
        [
            lax.dynamic_slice_in_dim(head_maps[0], core * (heads // 2), heads // 2),
            lax.dynamic_slice_in_dim(out_maps[0], core * (heads // 2), heads // 2),
        ],
        axis=2,
    )
    own = (params, weights)
    lift = [(spot(x, 0, a), spot(x, 1, b)) for x in range(1, planes) for a, b in climb]
    under_params, taken = lax.optimization_barrier((send(params, lift), taken))
    under = (jnp.where(plane > 0, under_params, params), send(weights, lift))
    kv, x0 = unfold(taken.reshape(seq_count * local, -1), half)

    def tail(x):
        return x[tokens:, :tokens]

    def join(x):
        return lax.all_gather(tail(x), "c", axis=0)

    def hop(x, pairs):
        arrived = send(x, pairs)
        swapped = [(2 * a + i, 2 * b + 1 - i) for a, b in pairs for i in range(2)]
        partner = lax.ppermute(tail(x), ("x", "yh", "yl", "c"), swapped)
        return (arrived, jnp.stack([tail(arrived), partner]))

    middle = tokens // 2
    x1 = jnp.concatenate(
        [
            send(part, [(spot(source, 0, y), spot(0, 0, y)) for y in (0, last)])
            for source, part in ((1, x0[:middle]), (planes - 1, x0[middle:]))
        ]
    )
    current = [(x0, join(x0)), (x1, None)]

    def piece(arrays, y):
        at = (z * yl_count + y) * span
        cuts = []
        for fresh, x in arrays:
            cuts += [
                lax.dynamic_slice_in_dim(fresh, at, span),
                lax.dynamic_slice_in_dim(fresh, tokens + at, span),
                lax.dynamic_slice_in_dim(x, at, span),
            ]
        return jnp.stack(cuts)

    beside, far = (jnp.where(low, 1, last - 1), jnp.where(low, last - 1, 1))
    across = jnp.where(low, last, 0)

    found = []
    for step in range(2):
        if step == 0:
            way = [(spot(0, 0, a), spot(0, 1, b)) for a, b in climb]
        else:
            way = [(spot(0, 1, y), spot(1, 1, y)) for y in (0, last)]
        done, other = ([], kv)
        for patch in range(2):
            came, stat = current[patch]
            if step or patch:
                came, x = lax.optimization_barrier((came, x))
            stat = join(came) if stat is None else stat
            x, other = block_step((0, step), came, stat, own, other)
            current[patch] = (send(x, way), None) if step else hop(x, way)
            if step == patch == 0:
                lifted, _ = lax.optimization_barrier((kv, x))
                under_kv = send(lifted, lift)
            done.append((other, x))
        found.append((piece(done, yl), piece(done, beside)))
    mine, near = [jnp.where(upper == 0, a, b) for a, b in zip(*found)]

    down = None
    for turn in range(1, planes):
        fresh = [under_kv, kv]
        done = [[], []]
        way = [(spot(turn, 1, y), spot(turn + 1, 1, y)) for y in (0, last)]
        for patch in range(2):
            came, x = lax.optimization_barrier((current[patch][0], x))
            x = came
            for index, block in enumerate((under, own)):
                x, fresh[index] = block_step((turn, 1), x, join(x), block, fresh[index])
                done[index].append((fresh[index], x))
            if turn < planes - 1:
                current[patch] = (send(x, way), None)
        here = plane == turn
        new = (piece(done[0], across), piece(done[0], far))
        down = new if down is None else [jnp.where(here, a, b) for a, b in zip(new, down)]
        mine = jnp.where(here, piece(done[1], yl), mine)
        near = jnp.where(here, piece(done[1], beside), near)

    inner = [(0, 1), (last, last - 1)]
    spread = [(spot(x, 1, a), spot(x, 1, b)) for x in range(planes) for a, b in inner]
    spread += [(spot(0, 0, a), spot(0, 0, b)) for a, b in inner]
    descend = [(spot(x, 1, a), spot(x, 0, b)) for x in range(1, planes) for a, b in climb]
    reach = [(0, last - 1), (last, 1)]
    beyond = [(spot(x, 1, a), spot(x, 0, b)) for x in range(1, planes) for a, b in reach]
    got = jnp.where(
        jnp.logical_or(plane == 0, upper == 1),
        send(near, spread),
        jnp.where(jnp.logical_or(low, yl == last), send(down[0], descend), send(down[1], beyond)),
    )
    local_site = jnp.logical_and(
        jnp.logical_or(plane == 0, upper == 1), jnp.logical_or(low, yl == last)
    )
    kept = jnp.where(local_site, mine, got)

    both = lax.all_gather(kept, "c", axis=0).reshape((-1,) + kept.shape[1:])
    block_out, fresh_out = settle(core[None].astype(jnp.int32), patch_rows, both)
    return (block_out[None], fresh_out[None])


def solution(mesh):
    fine = Mesh(mesh.devices.reshape(4, 2, 8, 4, 2), ("x", "yh", "z", "yl", "c"))
    section, seq = (("x", "yh"), SEQ)
    in_specs = (
        P(seq, None),
        P(section, None, None, None),
        P(section, None, None, None),
        P(section, None, None),
        P(section, None, None, None),
        P(section, None, seq, None),
        P(),
        P(seq),
        P(),
    )
    out_specs = (P(section, seq, None), P(section, seq, None))
    return jax.shard_map(shards, mesh=fine, in_specs=in_specs, out_specs=out_specs, check_vma=False)
```

```python
import functools
import math

import jax
import jax.numpy as jnp
from jax import lax
from jax.experimental import pallas as pl
from jax.experimental.pallas import tpu as pltpu
from jax.sharding import Mesh
from jax.sharding import PartitionSpec as P

HEAD_DIM = 128
EPS = 1e-06
QUERY_SCALE = HEAD_DIM ** (-0.5) * math.log2(math.e)
VMEM = pl.BlockSpec(memory_space=pltpu.VMEM)
STAT_ROWS = 16
SEQ = ("z", "yl", "c")
PARAMS = pltpu.CompilerParams(vmem_limit_bytes=32 * 2**20)


def row_to_columns(first, second):
    rows = lax.broadcasted_iota(jnp.int32, (HEAD_DIM, first.shape[1]), 0)
    return jnp.transpose(jnp.where(rows == 0, first, second))


def split_rows(row):
    parts = []
    for _ in range(3):
        part = row.astype(jnp.bfloat16).astype(jnp.float32)
        parts.append(part)
        row = row - part
    return parts


def half_stats(pieces):
    width = len(pieces) * HEAD_DIM
    total = pieces[0]
    for piece in pieces[1:]:
        total = total + piece
    center = jnp.sum(total, axis=1, keepdims=True) * (1.0 / width)
    squares = jnp.square(pieces[0] - center)
    for piece in pieces[1:]:
        squares = squares + jnp.square(piece - center)
    spread = jnp.sum(squares, axis=1, keepdims=True)
    lanes = lax.broadcasted_iota(jnp.int32, squares.shape, 1)
    both = jnp.transpose(jnp.where(lanes == 0, center, spread))
    rows = lax.broadcasted_iota(jnp.int32, (STAT_ROWS, both.shape[1]), 0)
    packed = jnp.zeros(rows.shape, jnp.float32)
    for index, part in enumerate(split_rows(both[0:1]) + split_rows(both[1:2])):
        packed = jnp.where(rows == index, part, packed)
    return packed.astype(jnp.bfloat16)


def head_slices(width):
    return [slice(h * HEAD_DIM, (h + 1) * HEAD_DIM) for h in range(width // HEAD_DIM)]


def offer_kernel(
    half_ref, age_hbm, rows_hbm, stale_hbm, stream_hbm, copies_hbm,
    age_ref, rows_ref, stale_ref, stream_ref, stale_rows, stream_rows, out_ref, piece_ref, sems,
    copy_sems,
):
    pairs = (
        (age_hbm, age_ref),
        (rows_hbm, rows_ref),
        (stale_hbm, stale_ref),
        (stream_hbm, stream_ref),
    )
    copies = [
        pltpu.make_async_copy(source, target, sems.at[i])
        for i, (source, target) in enumerate(pairs)
    ]
    for copy in copies:
        copy.start()
    for copy in copies:
        copy.wait()
    local = stream_ref.shape[0]
    rows = local // 2
    width = stream_ref.shape[1] // 2
    fold = 3 * width // 2
    rest = fold - width
    index = lax.broadcasted_iota(jnp.int32, (local, 1), 0)
    newer = jnp.zeros((local, 1), jnp.int32)
    for row in range(local):
        newer = jnp.where(index == row, age_ref[row], newer)
    stale_rows[...] = jnp.where(
        newer == 1, stale_ref[1].astype(jnp.float32), stale_ref[0].astype(jnp.float32)
    )
    stream_rows[...] = stream_ref[...].astype(jnp.float32)
    for row in range(rows):
        stale = stale_rows[pl.ds(rows_ref[rows + row], 1), :]
        stream = stream_rows[pl.ds(rows_ref[half_ref[0] * rows + row], 1), :]
        for core in range(2):
            keys = stale[:, core * width : (core + 1) * width]
            values = stale[:, (core + 2) * width : (core + 3) * width]
            out_ref[core, row : row + 1, :width] = keys
            out_ref[core, row : row + 1, width:] = values[:, :rest]
            out_ref[core, rows + row : rows + row + 1, : width - rest] = values[:, rest:]
            out_ref[core, rows + row : rows + row + 1, width - rest :] = stream[
                :, core * width : (core + 1) * width
            ]
    for core in range(2):
        piece_ref[core] = out_ref[core].astype(jnp.bfloat16)
    copies = [
        pltpu.make_async_copy(piece_ref, copies_hbm.at[pl.ds(2 * i, 2)], copy_sems.at[i])
        for i in range(copies_hbm.shape[0] // 2)
    ]
    for copy in copies:
        copy.start()
    for copy in copies:
        copy.wait()


def offer(patch, ages, patch_rows, stale, stream, count):
    local, width = stream.shape
    small = pl.BlockSpec(memory_space=pltpu.SMEM)
    return pl.pallas_call(
        offer_kernel,
        out_shape=jax.ShapeDtypeStruct((count, local, 3 * width // 4), jnp.bfloat16),
        in_specs=[small] + [pl.BlockSpec(memory_space=pltpu.HBM)] * 4,
        out_specs=pl.BlockSpec(memory_space=pltpu.HBM),
        scratch_shapes=[
            pltpu.SMEM(ages.shape, jnp.int32),
            pltpu.SMEM(patch_rows.shape, jnp.int32),
            pltpu.VMEM(stale.shape, stale.dtype),
            pltpu.VMEM(stream.shape, stream.dtype),
            pltpu.VMEM((local, 2 * width), jnp.float32),
            pltpu.VMEM((local, width), jnp.float32),
            pltpu.VMEM((2, local, 3 * width // 4), jnp.float32),
            pltpu.VMEM((2, local, 3 * width // 4), jnp.bfloat16),
            pltpu.SemaphoreType.DMA((4,)),
            pltpu.SemaphoreType.DMA((count // 2,)),
        ],
        compiler_params=pltpu.CompilerParams(vmem_limit_bytes=60 * 2**20),
        name="offer",
    )(patch, ages, patch_rows, stale, stream)


def unfold_kernel(taken_ref, kv_ref, x_ref):
    tokens, width = (kv_ref.shape[0] // 2, kv_ref.shape[1])
    rows, block = (4, 128)
    rest, part = (width // 2, block // 2)
    at = lax.broadcasted_iota(jnp.int32, (block, block), 0)
    column = lax.broadcasted_iota(jnp.int32, (block, block), 1)
    upper = lax.div(at, part)
    token = at - upper * part
    source = token + lax.div(token, rows) * rows + upper * rows
    pick = jnp.where(column == source, 1.0, 0.0).astype(jnp.bfloat16)
    for index in range(taken_ref.shape[0] // block):
        piece = taken_ref[index * block : (index + 1) * block, :]
        moved = jnp.dot(pick, piece, preferred_element_type=jnp.float32).astype(jnp.bfloat16)
        top, bottom = (moved[:part], moved[part:])
        first = slice(index * part, (index + 1) * part)
        second = slice(tokens + index * part, tokens + (index + 1) * part)
        kv_ref[first, :] = top[:, :width]
        kv_ref[second, :rest] = top[:, width:]
        kv_ref[second, rest:] = bottom[:, :rest]
        x_ref[first, :] = bottom[:, rest:]
    close_stream(x_ref, tokens)


def close_stream(x_ref, tokens):
    width = x_ref.shape[1]
    pieces = [x_ref[:tokens, cut].astype(jnp.float32) for cut in head_slices(width)]
    x_ref[tokens:, :tokens] = half_stats(pieces)
    x_ref[tokens:, tokens:] = jnp.zeros((STAT_ROWS, width - tokens), jnp.bfloat16)


def unfold(taken, width):
    tokens = taken.shape[0] // 2
    return pl.pallas_call(
        unfold_kernel,
        out_shape=(
            jax.ShapeDtypeStruct((2 * tokens, width), jnp.bfloat16),
            jax.ShapeDtypeStruct((tokens + STAT_ROWS, width), jnp.bfloat16),
        ),
        in_specs=[VMEM],
        out_specs=(VMEM,) * 2,
        compiler_params=PARAMS,
        name="unfold",
    )(taken)


def scores(left, right):
    return lax.dot_general(
        left, right, (((1,), (1,)), ((), ())), preferred_element_type=jnp.float32
    )


def unit_norm(part):
    return part * lax.rsqrt(jnp.mean(part * part, axis=1, keepdims=True) + EPS)


def settle_kernel(core_ref, rows_ref, both_ref, block_ref, fresh_ref, rows_in, rows_out):
    count, span, half = both_ref.shape
    rows = span // 2
    kinds = count // 4
    for index in range(count):
        rows_in[index] = both_ref[index].astype(jnp.float32)
    for patch in range(2):
        for row in range(rows):
            source = core_ref[0] * rows + row
            target = rows_ref[patch * rows + row]
            for core in range(2):
                for kind in range(kinds):
                    at = (kind * 2 + core) * half
                    index = (core * 2 + patch) * kinds + kind
                    rows_out[pl.ds(target, 1), at : at + half] = rows_in[
                        index, pl.ds(source, 1), :
                    ]
    cut = 4 * half
    fresh_ref[...] = rows_out[:, :cut].astype(jnp.bfloat16)
    block_ref[...] = rows_out[:, cut:].astype(jnp.bfloat16)


def settle(core, patch_rows, both):
    count, span, half = both.shape
    small = pl.BlockSpec(memory_space=pltpu.SMEM)
    return pl.pallas_call(
        settle_kernel,
        out_shape=(
            jax.ShapeDtypeStruct((span, 2 * half), jnp.bfloat16),
            jax.ShapeDtypeStruct((span, 4 * half), jnp.bfloat16),
        ),
        in_specs=[small] * 2 + [VMEM],
        out_specs=(VMEM,) * 2,
        scratch_shapes=[
            pltpu.VMEM(both.shape, jnp.float32),
            pltpu.VMEM((span, 6 * half), jnp.float32),
        ],
        compiler_params=PARAMS,
        name="settle",
    )(core, patch_rows, both)


def block_kernel(site, *refs):
    here = jnp.logical_and(lax.axis_index("x") == site[0], lax.axis_index("yh") == site[1])
    pl.when(here)(lambda: compute_block(*refs))


def compute_block(x_ref, st_ref, par_ref, w_ref, other_ref, xo_ref, kv_ref):
    tokens, width = (kv_ref.shape[0] // 2, kv_ref.shape[1])

    def joined(core, first):
        parts = [st_ref[core, first + i : first + i + 1].astype(jnp.float32) for i in range(3)]
        return parts[0] + parts[1] + parts[2]

    mean_a, mean_b = (joined(0, 0), joined(1, 0))
    spread = joined(0, 3) + joined(1, 3) + jnp.square(mean_a - mean_b) * (0.5 * width)
    columns = row_to_columns(
        0.5 * (mean_a + mean_b), lax.rsqrt(spread * (0.5 / width) + EPS)
    )
    mean = jnp.broadcast_to(columns[:, 0:1], (tokens, HEAD_DIM))
    rstd = jnp.broadcast_to(columns[:, 1:2], (tokens, HEAD_DIM))
    query_gain = par_ref[3:4, :HEAD_DIM] * QUERY_SCALE
    key_gain = par_ref[3:4, HEAD_DIM : 2 * HEAD_DIM]
    cuts = head_slices(width)

    def project(head):
        cut = cuts[head]
        x = x_ref[:tokens, cut].astype(jnp.float32)
        mod_in = (x - mean) * rstd * (1.0 + par_ref[1:2, cut]) + par_ref[0:1, cut]
        projected = jnp.dot(
            mod_in.astype(jnp.bfloat16),
            w_ref[head, :, : 3 * HEAD_DIM],
            preferred_element_type=jnp.float32,
        )
        query = (unit_norm(projected[:, :HEAD_DIM]) * query_gain).astype(jnp.bfloat16)
        key = (unit_norm(projected[:, HEAD_DIM : 2 * HEAD_DIM]) * key_gain).astype(jnp.bfloat16)
        value = projected[:, 2 * HEAD_DIM :].astype(jnp.bfloat16)
        kv_ref[:tokens, cut] = key
        kv_ref[tokens:, cut] = value
        return (query, key, value)

    def weigh(head, query, key, value):
        fresh = jnp.exp2(scores(query, key))
        other = jnp.exp2(scores(query, other_ref[:tokens, cuts[head]]))
        total = jnp.sum(fresh + other, axis=1, keepdims=True)
        return (fresh.astype(jnp.bfloat16), other.astype(jnp.bfloat16), total, value)

    def finish(head, fresh, other, total, value):
        cut = cuts[head]
        numerator = jnp.dot(fresh, value, preferred_element_type=jnp.float32) + jnp.dot(
            other, other_ref[tokens:, cut], preferred_element_type=jnp.float32
        )
        branch = jnp.dot(
            (numerator / total).astype(jnp.bfloat16),
            w_ref[head, :, 3 * HEAD_DIM :],
            preferred_element_type=jnp.float32,
        )
        x = x_ref[:tokens, cut].astype(jnp.float32)
        xo_ref[:tokens, cut] = (x + par_ref[2:3, cut] * branch).astype(jnp.bfloat16)

    parts = [project(head) for head in range(len(cuts))]
    ready = weigh(0, *parts[0])
    for head in range(len(cuts)):
        after = weigh(head + 1, *parts[head + 1]) if head + 1 < len(cuts) else None
        finish(head, *ready)
        ready = after
    close_stream(xo_ref, tokens)


def block_step(site, x, stats, block, other):
    params, weights = block
    return pl.pallas_call(
        functools.partial(block_kernel, site),
        out_shape=(
            jax.ShapeDtypeStruct(x.shape, jnp.bfloat16),
            jax.ShapeDtypeStruct(other.shape, jnp.bfloat16),
        ),
        in_specs=[VMEM] * 5,
        out_specs=(VMEM,) * 2,
        compiler_params=PARAMS,
        cost_estimate=pl.CostEstimate(
            flops=1_000_000, bytes_accessed=100_000, transcendentals=1_000
        ),
        name="block_step",
    )(x, stats, params, weights, other)


def shards(
    stream_in,
    head_maps,
    out_maps,
    norm_gains,
    modulation,
    stale_cache,
    patch_rows,
    stale_age,
    timestep,
):
    local, width = stream_in.shape
    heads = head_maps.shape[1]
    half = width // 2
    rows = local // 2
    span = 2 * rows
    planes, yl_count = (lax.axis_size("x"), lax.axis_size("yl"))
    z_count, seq_count = (lax.axis_size("z"), lax.axis_size(SEQ))
    core, plane, upper = (lax.axis_index("c"), lax.axis_index("x"), lax.axis_index("yh"))
    z, yl = (lax.axis_index("z"), lax.axis_index("yl"))
    tokens = seq_count * rows
    low = yl == 0

    def spot(x, yh, y):
        return (x * 2 + yh) * yl_count + y

    def send(array, pairs):
        return lax.ppermute(array, ("x", "yh", "yl"), pairs)

    last = yl_count - 1
    climb = [(0, last), (last, 0)]

    patch = jnp.where(plane == 0, 0, 1).astype(jnp.int32)
    given = offer(patch[None], stale_age, patch_rows, stale_cache[0], stream_in, seq_count)
    taken = lax.all_to_all(given, SEQ, split_axis=0, concat_axis=0, tiled=True)

    mod = lax.dynamic_index_in_dim(modulation[0], timestep[0], 0, keepdims=False)
    mod = lax.dynamic_slice_in_dim(mod, core * half, half, axis=1)
    gains = jnp.pad(norm_gains[0].reshape(1, 2 * HEAD_DIM), ((0, 0), (0, half - 2 * HEAD_DIM)))
    params = jnp.concatenate([mod, gains], axis=0)
    weights = jnp.concatenate(
        [
            lax.dynamic_slice_in_dim(head_maps[0], core * (heads // 2), heads // 2),
            lax.dynamic_slice_in_dim(out_maps[0], core * (heads // 2), heads // 2),
        ],
        axis=2,
    )
    own = (params, weights)
    lift = [(spot(x, 0, a), spot(x, 1, b)) for x in range(1, planes) for a, b in climb]
    under_params, taken = lax.optimization_barrier((send(params, lift), taken))
    under = (jnp.where(plane > 0, under_params, params), send(weights, lift))
    kv, x0 = unfold(taken.reshape(seq_count * local, -1), half)

    def tail(x):
        return x[tokens:, :tokens]

    def join(x):
        return lax.all_gather(tail(x), "c", axis=0)

    def hop(x, pairs):
        arrived = send(x, pairs)
        swapped = [(2 * a + i, 2 * b + 1 - i) for a, b in pairs for i in range(2)]
        partner = lax.ppermute(tail(x), ("x", "yh", "yl", "c"), swapped)
        return (arrived, jnp.stack([tail(arrived), partner]))

    across_planes = [(spot(1, 0, y), spot(0, 0, y)) for y in (0, last)]
    current = [(x0, join(x0)), (send(x0, across_planes), None)]

    def piece(arrays, y):
        at = (z * yl_count + y) * span
        cuts = []
        for fresh, x in arrays:
            cuts += [
                lax.dynamic_slice_in_dim(fresh, at, span),
                lax.dynamic_slice_in_dim(fresh, tokens + at, span),
                lax.dynamic_slice_in_dim(x, at, span),
            ]
        return jnp.stack(cuts)

    beside, far = (jnp.where(low, 1, last - 1), jnp.where(low, last - 1, 1))
    across = jnp.where(low, last, 0)

    found = []
    for step in range(2):
        if step == 0:
            way = [(spot(0, 0, a), spot(0, 1, b)) for a, b in climb]
        else:
            way = [(spot(0, 1, y), spot(1, 1, y)) for y in (0, last)]
        done, other = ([], kv)
        for patch in range(2):
            came, stat = current[patch]
            if step or patch:
                came, x = lax.optimization_barrier((came, x))
            stat = join(came) if stat is None else stat
            x, other = block_step((0, step), came, stat, own, other)
            current[patch] = (send(x, way), None) if step else hop(x, way)
            if step == patch == 0:
                lifted, _ = lax.optimization_barrier((kv, x))
                under_kv = send(lifted, lift)
            done.append((other, x))
        found.append((piece(done, yl), piece(done, beside)))
    mine, near = [jnp.where(upper == 0, a, b) for a, b in zip(*found)]

    down = None
    for turn in range(1, planes):
        fresh = [under_kv, kv]
        done = [[], []]
        way = [(spot(turn, 1, y), spot(turn + 1, 1, y)) for y in (0, last)]
        for patch in range(2):
            came, x = lax.optimization_barrier((current[patch][0], x))
            x = came
            for index, block in enumerate((under, own)):
                x, fresh[index] = block_step((turn, 1), x, join(x), block, fresh[index])
                done[index].append((fresh[index], x))
            if turn < planes - 1:
                current[patch] = (send(x, way), None)
        here = plane == turn
        new = (piece(done[0], across), piece(done[0], far))
        down = new if down is None else [jnp.where(here, a, b) for a, b in zip(new, down)]
        mine = jnp.where(here, piece(done[1], yl), mine)
        near = jnp.where(here, piece(done[1], beside), near)

    inner = [(0, 1), (last, last - 1)]
    spread = [(spot(x, 1, a), spot(x, 1, b)) for x in range(planes) for a, b in inner]
    spread += [(spot(0, 0, a), spot(0, 0, b)) for a, b in inner]
    descend = [(spot(x, 1, a), spot(x, 0, b)) for x in range(1, planes) for a, b in climb]
    reach = [(0, last - 1), (last, 1)]
    beyond = [(spot(x, 1, a), spot(x, 0, b)) for x in range(1, planes) for a, b in reach]
    got = jnp.where(
        jnp.logical_or(plane == 0, upper == 1),
        send(near, spread),
        jnp.where(jnp.logical_or(low, yl == last), send(down[0], descend), send(down[1], beyond)),
    )
    local_site = jnp.logical_and(
        jnp.logical_or(plane == 0, upper == 1), jnp.logical_or(low, yl == last)
    )
    kept = jnp.where(local_site, mine, got)

    both = lax.all_gather(kept, "c", axis=0).reshape((-1,) + kept.shape[1:])
    block_out, fresh_out = settle(core[None].astype(jnp.int32), patch_rows, both)
    return (block_out[None], fresh_out[None])


def solution(mesh):
    fine = Mesh(mesh.devices.reshape(4, 2, 8, 4, 2), ("x", "yh", "z", "yl", "c"))
    section, seq = (("x", "yh"), SEQ)
    in_specs = (
        P(seq, None),
        P(section, None, None, None),
        P(section, None, None, None),
        P(section, None, None),
        P(section, None, None, None),
        P(section, None, seq, None),
        P(),
        P(seq),
        P(),
    )
    out_specs = (P(section, seq, None), P(section, seq, None))
    return jax.shard_map(shards, mesh=fine, in_specs=in_specs, out_specs=out_specs, check_vma=False)
```

```python
import functools
import math

import jax
import jax.numpy as jnp
from jax import lax
from jax.experimental import pallas as pl
from jax.experimental.pallas import tpu as pltpu
from jax.sharding import Mesh
from jax.sharding import PartitionSpec as P

HEAD_DIM = 128
EPS = 1e-06
QUERY_SCALE = HEAD_DIM ** (-0.5) * math.log2(math.e)
VMEM = pl.BlockSpec(memory_space=pltpu.VMEM)
STAT_ROWS = 16
SEQ = ("z", "yl", "c")
PARAMS = pltpu.CompilerParams(vmem_limit_bytes=32 * 2**20)


def row_to_columns(first, second):
    rows = lax.broadcasted_iota(jnp.int32, (HEAD_DIM, first.shape[1]), 0)
    return jnp.transpose(jnp.where(rows == 0, first, second))


def split_rows(row):
    parts = []
    for _ in range(3):
        part = row.astype(jnp.bfloat16).astype(jnp.float32)
        parts.append(part)
        row = row - part
    return parts


def half_stats(pieces):
    width = len(pieces) * HEAD_DIM
    total = pieces[0]
    for piece in pieces[1:]:
        total = total + piece
    center = jnp.sum(total, axis=1, keepdims=True) * (1.0 / width)
    squares = jnp.square(pieces[0] - center)
    for piece in pieces[1:]:
        squares = squares + jnp.square(piece - center)
    spread = jnp.sum(squares, axis=1, keepdims=True)
    lanes = lax.broadcasted_iota(jnp.int32, squares.shape, 1)
    both = jnp.transpose(jnp.where(lanes == 0, center, spread))
    rows = lax.broadcasted_iota(jnp.int32, (STAT_ROWS, both.shape[1]), 0)
    packed = jnp.zeros(rows.shape, jnp.float32)
    for index, part in enumerate(split_rows(both[0:1]) + split_rows(both[1:2])):
        packed = jnp.where(rows == index, part, packed)
    return packed.astype(jnp.bfloat16)


def head_slices(width):
    return [slice(h * HEAD_DIM, (h + 1) * HEAD_DIM) for h in range(width // HEAD_DIM)]


def offer_kernel(
    half_ref, age_hbm, rows_hbm, stale_hbm, stream_hbm, copies_hbm,
    age_ref, rows_ref, stale_ref, stream_ref, stale_rows, stream_rows, out_ref, piece_ref, sems,
    copy_sems,
):
    pairs = (
        (age_hbm, age_ref),
        (rows_hbm, rows_ref),
        (stale_hbm, stale_ref),
        (stream_hbm, stream_ref),
    )
    copies = [
        pltpu.make_async_copy(source, target, sems.at[i])
        for i, (source, target) in enumerate(pairs)
    ]
    for copy in copies:
        copy.start()
    for copy in copies:
        copy.wait()
    local = stream_ref.shape[0]
    rows = local // 2
    width = stream_ref.shape[1] // 2
    fold = 3 * width // 2
    rest = fold - width
    index = lax.broadcasted_iota(jnp.int32, (local, 1), 0)
    newer = jnp.zeros((local, 1), jnp.int32)
    for row in range(local):
        newer = jnp.where(index == row, age_ref[row], newer)
    stale_rows[...] = jnp.where(
        newer == 1, stale_ref[1].astype(jnp.float32), stale_ref[0].astype(jnp.float32)
    )
    stream_rows[...] = stream_ref[...].astype(jnp.float32)
    for row in range(rows):
        stale = stale_rows[pl.ds(rows_ref[rows + row], 1), :]
        stream = stream_rows[pl.ds(rows_ref[half_ref[0] * rows + row], 1), :]
        for core in range(2):
            keys = stale[:, core * width : (core + 1) * width]
            values = stale[:, (core + 2) * width : (core + 3) * width]
            out_ref[core, row : row + 1, :width] = keys
            out_ref[core, row : row + 1, width:] = values[:, :rest]
            out_ref[core, rows + row : rows + row + 1, : width - rest] = values[:, rest:]
            out_ref[core, rows + row : rows + row + 1, width - rest :] = stream[
                :, core * width : (core + 1) * width
            ]
    for core in range(2):
        piece_ref[core] = out_ref[core].astype(jnp.bfloat16)
    copies = [
        pltpu.make_async_copy(piece_ref, copies_hbm.at[pl.ds(2 * i, 2)], copy_sems.at[i])
        for i in range(copies_hbm.shape[0] // 2)
    ]
    for copy in copies:
        copy.start()
    for copy in copies:
        copy.wait()


def offer(patch, ages, patch_rows, stale, stream, count):
    local, width = stream.shape
    small = pl.BlockSpec(memory_space=pltpu.SMEM)
    return pl.pallas_call(
        offer_kernel,
        out_shape=jax.ShapeDtypeStruct((count, local, 3 * width // 4), jnp.bfloat16),
        in_specs=[small] + [pl.BlockSpec(memory_space=pltpu.HBM)] * 4,
        out_specs=pl.BlockSpec(memory_space=pltpu.HBM),
        scratch_shapes=[
            pltpu.SMEM(ages.shape, jnp.int32),
            pltpu.SMEM(patch_rows.shape, jnp.int32),
            pltpu.VMEM(stale.shape, stale.dtype),
            pltpu.VMEM(stream.shape, stream.dtype),
            pltpu.VMEM((local, 2 * width), jnp.float32),
            pltpu.VMEM((local, width), jnp.float32),
            pltpu.VMEM((2, local, 3 * width // 4), jnp.float32),
            pltpu.VMEM((2, local, 3 * width // 4), jnp.bfloat16),
            pltpu.SemaphoreType.DMA((4,)),
            pltpu.SemaphoreType.DMA((count // 2,)),
        ],
        compiler_params=pltpu.CompilerParams(vmem_limit_bytes=60 * 2**20),
        name="offer",
    )(patch, ages, patch_rows, stale, stream)


def pieces(taken_ref, columns, keep):
    rows, block = (4, 128)
    part = block // 2
    at = lax.broadcasted_iota(jnp.int32, (block if keep is None else part, block), 0)
    column = lax.broadcasted_iota(jnp.int32, at.shape, 1)
    half = lax.div(at, part) if keep is None else keep
    token = at - half * part if keep is None else at
    source = token + lax.div(token, rows) * rows + half * rows
    pick = jnp.where(column == source, 1.0, 0.0).astype(jnp.bfloat16)
    for index in range(taken_ref.shape[0] // block):
        piece = taken_ref[index * block : (index + 1) * block, columns]
        moved = jnp.dot(pick, piece, preferred_element_type=jnp.float32).astype(jnp.bfloat16)
        yield (slice(index * part, (index + 1) * part), moved)


def stream_kernel(taken_ref, x_ref):
    width = x_ref.shape[1]
    for rows, moved in pieces(taken_ref, slice(width // 2, None), 1):
        x_ref[rows, :] = moved
    close_stream(x_ref, x_ref.shape[0] - STAT_ROWS)


def stale_kernel(taken_ref, kv_ref):
    tokens, width = (kv_ref.shape[0] // 2, kv_ref.shape[1])
    rest = width // 2
    for rows, moved in pieces(taken_ref, slice(None), None):
        part = rows.stop - rows.start
        second = slice(tokens + rows.start, tokens + rows.stop)
        kv_ref[rows, :] = moved[:part, :width]
        kv_ref[second, :rest] = moved[:part, width:]
        kv_ref[second, rest:] = moved[part:, :rest]


def close_stream(x_ref, tokens):
    width = x_ref.shape[1]
    pieces = [x_ref[:tokens, cut].astype(jnp.float32) for cut in head_slices(width)]
    x_ref[tokens:, :tokens] = half_stats(pieces)
    x_ref[tokens:, tokens:] = jnp.zeros((STAT_ROWS, width - tokens), jnp.bfloat16)


def unfold(kernel, taken, shape, name):
    return pl.pallas_call(
        kernel,
        out_shape=jax.ShapeDtypeStruct(shape, jnp.bfloat16),
        in_specs=[VMEM],
        out_specs=VMEM,
        compiler_params=PARAMS,
        name=name,
    )(taken)


def scores(left, right):
    return lax.dot_general(
        left, right, (((1,), (1,)), ((), ())), preferred_element_type=jnp.float32
    )


def unit_norm(part):
    return part * lax.rsqrt(jnp.mean(part * part, axis=1, keepdims=True) + EPS)


def settle_kernel(core_ref, rows_ref, both_ref, block_ref, fresh_ref, rows_in, rows_out):
    count, span, half = both_ref.shape
    rows = span // 2
    kinds = count // 4
    for index in range(count):
        rows_in[index] = both_ref[index].astype(jnp.float32)
    for patch in range(2):
        for row in range(rows):
            source = core_ref[0] * rows + row
            target = rows_ref[patch * rows + row]
            for core in range(2):
                for kind in range(kinds):
                    at = (kind * 2 + core) * half
                    index = (core * 2 + patch) * kinds + kind
                    rows_out[pl.ds(target, 1), at : at + half] = rows_in[
                        index, pl.ds(source, 1), :
                    ]
    cut = 4 * half
    fresh_ref[...] = rows_out[:, :cut].astype(jnp.bfloat16)
    block_ref[...] = rows_out[:, cut:].astype(jnp.bfloat16)


def settle(core, patch_rows, both):
    count, span, half = both.shape
    small = pl.BlockSpec(memory_space=pltpu.SMEM)
    return pl.pallas_call(
        settle_kernel,
        out_shape=(
            jax.ShapeDtypeStruct((span, 2 * half), jnp.bfloat16),
            jax.ShapeDtypeStruct((span, 4 * half), jnp.bfloat16),
        ),
        in_specs=[small] * 2 + [VMEM],
        out_specs=(VMEM,) * 2,
        scratch_shapes=[
            pltpu.VMEM(both.shape, jnp.float32),
            pltpu.VMEM((span, 6 * half), jnp.float32),
        ],
        compiler_params=PARAMS,
        name="settle",
    )(core, patch_rows, both)


def block_kernel(site, *refs):
    here = jnp.logical_and(lax.axis_index("x") == site[0], lax.axis_index("yh") == site[1])
    pl.when(here)(lambda: compute_block(*refs))


def compute_block(x_ref, st_ref, par_ref, w_ref, other_ref, xo_ref, kv_ref):
    tokens, width = (kv_ref.shape[0] // 2, kv_ref.shape[1])

    def joined(core, first):
        parts = [st_ref[core, first + i : first + i + 1].astype(jnp.float32) for i in range(3)]
        return parts[0] + parts[1] + parts[2]

    mean_a, mean_b = (joined(0, 0), joined(1, 0))
    spread = joined(0, 3) + joined(1, 3) + jnp.square(mean_a - mean_b) * (0.5 * width)
    columns = row_to_columns(
        0.5 * (mean_a + mean_b), lax.rsqrt(spread * (0.5 / width) + EPS)
    )
    mean = jnp.broadcast_to(columns[:, 0:1], (tokens, HEAD_DIM))
    rstd = jnp.broadcast_to(columns[:, 1:2], (tokens, HEAD_DIM))
    query_gain = par_ref[3:4, :HEAD_DIM] * QUERY_SCALE
    key_gain = par_ref[3:4, HEAD_DIM : 2 * HEAD_DIM]
    cuts = head_slices(width)

    def project(head):
        cut = cuts[head]
        x = x_ref[:tokens, cut].astype(jnp.float32)
        mod_in = (x - mean) * rstd * (1.0 + par_ref[1:2, cut]) + par_ref[0:1, cut]
        projected = jnp.dot(
            mod_in.astype(jnp.bfloat16),
            w_ref[head, :, : 3 * HEAD_DIM],
            preferred_element_type=jnp.float32,
        )
        query = (unit_norm(projected[:, :HEAD_DIM]) * query_gain).astype(jnp.bfloat16)
        key = (unit_norm(projected[:, HEAD_DIM : 2 * HEAD_DIM]) * key_gain).astype(jnp.bfloat16)
        value = projected[:, 2 * HEAD_DIM :].astype(jnp.bfloat16)
        kv_ref[:tokens, cut] = key
        kv_ref[tokens:, cut] = value
        return (query, key, value)

    def weigh(head, query, key, value):
        fresh = jnp.exp2(scores(query, key))
        other = jnp.exp2(scores(query, other_ref[:tokens, cuts[head]]))
        total = jnp.sum(fresh + other, axis=1, keepdims=True)
        return (fresh.astype(jnp.bfloat16), other.astype(jnp.bfloat16), total, value)

    def finish(head, fresh, other, total, value):
        cut = cuts[head]
        numerator = jnp.dot(fresh, value, preferred_element_type=jnp.float32) + jnp.dot(
            other, other_ref[tokens:, cut], preferred_element_type=jnp.float32
        )
        branch = jnp.dot(
            (numerator / total).astype(jnp.bfloat16),
            w_ref[head, :, 3 * HEAD_DIM :],
            preferred_element_type=jnp.float32,
        )
        x = x_ref[:tokens, cut].astype(jnp.float32)
        xo_ref[:tokens, cut] = (x + par_ref[2:3, cut] * branch).astype(jnp.bfloat16)

    parts = [project(head) for head in range(len(cuts))]
    ready = weigh(0, *parts[0])
    for head in range(len(cuts)):
        after = weigh(head + 1, *parts[head + 1]) if head + 1 < len(cuts) else None
        finish(head, *ready)
        ready = after
    close_stream(xo_ref, tokens)


def block_step(site, x, stats, block, other):
    params, weights = block
    return pl.pallas_call(
        functools.partial(block_kernel, site),
        out_shape=(
            jax.ShapeDtypeStruct(x.shape, jnp.bfloat16),
            jax.ShapeDtypeStruct(other.shape, jnp.bfloat16),
        ),
        in_specs=[VMEM] * 5,
        out_specs=(VMEM,) * 2,
        compiler_params=PARAMS,
        cost_estimate=pl.CostEstimate(
            flops=1_000_000, bytes_accessed=100_000, transcendentals=1_000
        ),
        name="block_step",
    )(x, stats, params, weights, other)


def shards(
    stream_in,
    head_maps,
    out_maps,
    norm_gains,
    modulation,
    stale_cache,
    patch_rows,
    stale_age,
    timestep,
):
    local, width = stream_in.shape
    heads = head_maps.shape[1]
    half = width // 2
    rows = local // 2
    span = 2 * rows
    planes, yl_count = (lax.axis_size("x"), lax.axis_size("yl"))
    z_count, seq_count = (lax.axis_size("z"), lax.axis_size(SEQ))
    core, plane, upper = (lax.axis_index("c"), lax.axis_index("x"), lax.axis_index("yh"))
    z, yl = (lax.axis_index("z"), lax.axis_index("yl"))
    tokens = seq_count * rows
    low = yl == 0

    def spot(x, yh, y):
        return (x * 2 + yh) * yl_count + y

    def send(array, pairs):
        return lax.ppermute(array, ("x", "yh", "yl"), pairs)

    last = yl_count - 1
    climb = [(0, last), (last, 0)]

    patch = jnp.where(plane == 0, 0, 1).astype(jnp.int32)
    given = offer(patch[None], stale_age, patch_rows, stale_cache[0], stream_in, seq_count)
    taken = lax.all_to_all(given, SEQ, split_axis=0, concat_axis=0, tiled=True)

    mod = lax.dynamic_index_in_dim(modulation[0], timestep[0], 0, keepdims=False)
    mod = lax.dynamic_slice_in_dim(mod, core * half, half, axis=1)
    gains = jnp.pad(norm_gains[0].reshape(1, 2 * HEAD_DIM), ((0, 0), (0, half - 2 * HEAD_DIM)))
    params = jnp.concatenate([mod, gains], axis=0)
    weights = jnp.concatenate(
        [
            lax.dynamic_slice_in_dim(head_maps[0], core * (heads // 2), heads // 2),
            lax.dynamic_slice_in_dim(out_maps[0], core * (heads // 2), heads // 2),
        ],
        axis=2,
    )
    own = (params, weights)
    lift = [(spot(x, 0, a), spot(x, 1, b)) for x in range(1, planes) for a, b in climb]
    under_params, taken = lax.optimization_barrier((send(params, lift), taken))
    under = (jnp.where(plane > 0, under_params, params), send(weights, lift))
    taken = taken.reshape(seq_count * local, -1)
    x0 = unfold(stream_kernel, taken, (tokens + STAT_ROWS, half), "unfold_stream")

    def tail(x):
        return x[tokens:, :tokens]

    def join(x):
        return lax.all_gather(tail(x), "c", axis=0)

    def hop(x, pairs):
        arrived = send(x, pairs)
        swapped = [(2 * a + i, 2 * b + 1 - i) for a, b in pairs for i in range(2)]
        partner = lax.ppermute(tail(x), ("x", "yh", "yl", "c"), swapped)
        return (arrived, jnp.stack([tail(arrived), partner]))

    across_planes = [(spot(1, 0, y), spot(0, 0, y)) for y in (0, last)]
    crossed, (taken, stat) = (
        send(x0, across_planes), lax.optimization_barrier((taken, join(x0))))
    kv = unfold(stale_kernel, taken, (2 * tokens, half), "unfold_stale")
    current = [(x0, stat), (crossed, None)]

    def piece(arrays, y):
        at = (z * yl_count + y) * span
        cuts = []
        for fresh, x in arrays:
            cuts += [
                lax.dynamic_slice_in_dim(fresh, at, span),
                lax.dynamic_slice_in_dim(fresh, tokens + at, span),
                lax.dynamic_slice_in_dim(x, at, span),
            ]
        return jnp.stack(cuts)

    beside, far = (jnp.where(low, 1, last - 1), jnp.where(low, last - 1, 1))
    across = jnp.where(low, last, 0)

    found = []
    for step in range(2):
        if step == 0:
            way = [(spot(0, 0, a), spot(0, 1, b)) for a, b in climb]
        else:
            way = [(spot(0, 1, y), spot(1, 1, y)) for y in (0, last)]
        done, other = ([], kv)
        for patch in range(2):
            came, stat = current[patch]
            if step or patch:
                came, x = lax.optimization_barrier((came, x))
            stat = join(came) if stat is None else stat
            x, other = block_step((0, step), came, stat, own, other)
            current[patch] = (send(x, way), None) if step else hop(x, way)
            if step == patch == 0:
                lifted, _ = lax.optimization_barrier((kv, x))
                under_kv = send(lifted, lift)
            done.append((other, x))
        found.append((piece(done, yl), piece(done, beside)))
    mine, near = [jnp.where(upper == 0, a, b) for a, b in zip(*found)]

    down = None
    for turn in range(1, planes):
        fresh = [under_kv, kv]
        done = [[], []]
        way = [(spot(turn, 1, y), spot(turn + 1, 1, y)) for y in (0, last)]
        for patch in range(2):
            came, x = lax.optimization_barrier((current[patch][0], x))
            x = came
            for index, block in enumerate((under, own)):
                x, fresh[index] = block_step((turn, 1), x, join(x), block, fresh[index])
                done[index].append((fresh[index], x))
            if turn < planes - 1:
                current[patch] = (send(x, way), None)
        here = plane == turn
        new = (piece(done[0], across), piece(done[0], far))
        down = new if down is None else [jnp.where(here, a, b) for a, b in zip(new, down)]
        mine = jnp.where(here, piece(done[1], yl), mine)
        near = jnp.where(here, piece(done[1], beside), near)

    inner = [(0, 1), (last, last - 1)]
    spread = [(spot(x, 1, a), spot(x, 1, b)) for x in range(planes) for a, b in inner]
    spread += [(spot(0, 0, a), spot(0, 0, b)) for a, b in inner]
    descend = [(spot(x, 1, a), spot(x, 0, b)) for x in range(1, planes) for a, b in climb]
    reach = [(0, last - 1), (last, 1)]
    beyond = [(spot(x, 1, a), spot(x, 0, b)) for x in range(1, planes) for a, b in reach]
    got = jnp.where(
        jnp.logical_or(plane == 0, upper == 1),
        send(near, spread),
        jnp.where(jnp.logical_or(low, yl == last), send(down[0], descend), send(down[1], beyond)),
    )
    local_site = jnp.logical_and(
        jnp.logical_or(plane == 0, upper == 1), jnp.logical_or(low, yl == last)
    )
    kept = jnp.where(local_site, mine, got)

    both = lax.all_gather(kept, "c", axis=0).reshape((-1,) + kept.shape[1:])
    block_out, fresh_out = settle(core[None].astype(jnp.int32), patch_rows, both)
    return (block_out[None], fresh_out[None])


def solution(mesh):
    fine = Mesh(mesh.devices.reshape(4, 2, 8, 4, 2), ("x", "yh", "z", "yl", "c"))
    section, seq = (("x", "yh"), SEQ)
    in_specs = (
        P(seq, None),
        P(section, None, None, None),
        P(section, None, None, None),
        P(section, None, None),
        P(section, None, None, None),
        P(section, None, seq, None),
        P(),
        P(seq),
        P(),
    )
    out_specs = (P(section, seq, None), P(section, seq, None))
    return jax.shard_map(shards, mesh=fine, in_specs=in_specs, out_specs=out_specs, check_vma=False)
```
